512 devices in a mesh: patch: 32 (over y_lo, z), head: 16 (over y_hi, x, core).
Axes of the slice: x: 4, y: 4 (y_hi: 2, y_lo: 2; y = y_hi * 2 + y_lo), z: 16, core: 2. Of those that a mesh axis runs over, the one named last changes fastest.
Arguments:
- state: float32 [4096, 3072], P('patch', 'head'), may hold values from -6 to 6
- mod_weight: bfloat16 [256, 2, 3072], P(None, None, 'head'), may hold values from -0.375 to 0.375
- w_qkv: bfloat16 [3072, 16, 384], P('patch', 'head'), may hold values from -0.109375 to 0.109375
- q_gain: float32 [16, 128], P('head'), as said below
- k_gain: float32 [16, 128], P('head'), may hold values from 1 to 4
- w_in: bfloat16 [3072, 6144], P('patch', 'head'), may hold values from -0.109375 to 0.109375
- w_attn: bfloat16 [2048, 3072], P('head', 'patch'), may hold values from -0.125 to 0.125
- w_out: bfloat16 [6144, 3072], P('head', 'patch'), may hold values from -0.078125 to 0.078125
- cache_keys: bfloat16 [4096, 16, 128], P(None, 'head'), may hold values from -200 to 200
- cache_values: bfloat16 [4096, 16, 128], P(None, 'head'), may hold values from -6 to 6
- timesteps: int32 [4], replicated, may hold values from 0 to 999, as said below
Outputs:
- final_state: float32 [4096, 3072], P('patch', 'head')
The draws below stay inside these ranges and needn't reach their ends.
Inputs may be any that keep to these rules, and one draw needn't show every extreme that they name: `timesteps`: rises by the same stride from each entry to the next, the stride at least 125; the last entry is 999. `q_gain`: positive.
All inputs are finite; a program needn't handle non-finite values.
Results may differ from the reference program's by a relative error of at most 0.04.
Values may be sent and summed in bfloat16 or wider, within the bound.
A program may use at most 64 MiB of HBM per device.

```python
import math
import jax
import jax.numpy as jnp
from jax import lax

D = 3072
HD = 128
HEAD_DEV = 1
HEADS = 16
FF = 6144
EMB = 256
SCHED = 1000
STEPS = 3
TOK_DEV = 128
TOKENS = 4096
N_PATCH = 32
N_HEAD = 16


def draw_timesteps(key, part):
    key = jax.random.fold_in(key, 11)
    stride = jax.random.randint(key, (), SCHED // 8, SCHED // 4 + 1)
    last = SCHED - 1
    return (last - stride * (STEPS - jnp.arange(STEPS + 1))).astype(jnp.int32)


def draw_q_gain(key, part):
    key = jax.random.fold_in(key, 12)
    lower, upper = (math.log(1.0), math.log(4.0))
    return jnp.exp(jax.random.uniform(key, (HEADS, HD), jnp.float32, lower, upper))


def draw_cache_keys(key, part):
    key = jax.random.fold_in(key, 13)
    first = jax.random.fold_in(key, 0)
    base = jnp.clip(jax.random.normal(first, (TOKENS, HEADS, HD), jnp.float32), -6.0, 6.0)
    return base.astype(jnp.bfloat16)


def levels(rng, shape, pieces, smallest, top_value):
    def one(axis_at, shards_of):
        draws = jax.random.uniform(jax.random.fold_in(jax.random.fold_in(rng, 6), axis_at), (shards_of,), jnp.float32, smallest / len(pieces), top_value / len(pieces))
        return jnp.repeat(jnp.exp(draws), shape[axis_at] // shards_of).reshape((-1,) + (1,) * (len(shape) - axis_at - 1))

    level = one(*pieces[0])
    for cut in pieces[1:]:
        level = level * one(*cut)
    return level


def bell_draw(stream_key, shape, width, reach, cuts=(), kind=jnp.bfloat16):
    drawn = jax.random.normal(stream_key, shape, jnp.float32) * width
    if len(cuts) > 0:
        drawn = levels(stream_key, shape, cuts, -0.22, 0.18) * drawn
    return jnp.clip(drawn, min=-reach, max=reach).astype(kind)


def setup_inputs(seed: int = 0) -> dict:
    key_list = jax.random.split(jax.random.key(seed), 12)
    state = bell_draw(key_list[0], (TOKENS, D), 1.0, 6.0, ((0, 32), (1, 16)), jnp.float32)
    mod_weight = bell_draw(key_list[1], (EMB, 2, D), EMB ** -0.5, 0.375, ((2, 16),))
    w_qkv = bell_draw(key_list[2], (D, HEADS, 3 * HD), D ** -0.5, 0.109375, ((0, 32), (1, 16)))
    q_gain = draw_q_gain(jax.random.fold_in(key_list[11], 71), 0)
    k_gain = jnp.clip(jnp.exp(math.log(4.0) - 1.3862944 * jax.random.uniform(key_list[4], (HEADS, HD), jnp.float32) ** levels(key_list[4], (HEADS, HD), ((0, 16),), -0.2, 0.2)), 1.0, 4.0)
    w_in = bell_draw(key_list[5], (D, FF), D ** -0.5, 0.109375, ((0, 32), (1, 16)))
    w_attn = bell_draw(key_list[6], (HEADS * HD, D), (HEADS * HD) ** -0.5, 0.125, ((0, 16), (1, 32)))
    w_out = bell_draw(key_list[7], (FF, D), FF ** -0.5, 0.078125, ((0, 16), (1, 32)))
    cache_keys = draw_cache_keys(jax.random.fold_in(key_list[11], 71), 0)
    cache_values = bell_draw(key_list[9], (TOKENS, HEADS, HD), 1.0, 6.0, ((1, 16),))
    timesteps = draw_timesteps(jax.random.fold_in(key_list[11], 71), 0)
    return {"state": state, "mod_weight": mod_weight, "w_qkv": w_qkv, "q_gain": q_gain, "k_gain": k_gain, "w_in": w_in, "w_attn": w_attn, "w_out": w_out, "cache_keys": cache_keys, "cache_values": cache_values, "timesteps": timesteps}


def sigma_of(index):
    unit = 1.0 - index.astype(jnp.float32) / SCHED
    return 3.0 * unit / (1.0 + 2.0 * unit)

def embed(level):
    half = EMB // 2
    freq = jnp.exp(-math.log(10000.0) * jnp.arange(half, dtype=jnp.float32) / half)
    angle = 1000.0 * level * freq
    return jnp.concatenate([jnp.cos(angle), jnp.sin(angle)]).astype(jnp.bfloat16)

def rms_scale(values, gain):
    return values * lax.rsqrt(lax.optimization_barrier(jnp.mean(values * values, -1, keepdims=True)) + 1e-06) * gain

def reference(state, mod_weight, w_qkv, q_gain, k_gain, w_in, w_attn, w_out, cache_keys, cache_values, timesteps):
    x = state
    keys_cache = cache_keys
    values_cache = cache_values
    ffd = FF // N_HEAD
    group = HEAD_DEV * HD
    for step in range(STEPS):
        level_a = sigma_of(timesteps[step])
        level_b = sigma_of(timesteps[step + 1])
        emb = embed(level_a)
        mod = jnp.dot(emb[None, :], mod_weight.reshape(EMB, 2 * D), preferred_element_type=jnp.float32).reshape(2, D)
        mean = lax.optimization_barrier(jnp.mean(x, -1, keepdims=True))
        var = lax.optimization_barrier(jnp.mean((x - mean) ** 2, -1, keepdims=True))
        h = ((x - mean) * lax.rsqrt(var + 1e-06) * (1.0 + mod[0]) + mod[1]).astype(jnp.bfloat16)
        qkv = jnp.dot(h, w_qkv.reshape(D, HEADS * 3 * HD), preferred_element_type=jnp.float32).reshape(TOKENS, HEADS, 3 * HD)
        query = rms_scale(qkv[..., :HD], q_gain).astype(jnp.bfloat16)
        key_new = rms_scale(qkv[..., HD:2 * HD], k_gain).astype(jnp.bfloat16)
        value_new = qkv[..., 2 * HD:].astype(jnp.bfloat16)

        def block(index):
            start = (index * TOK_DEV).astype(jnp.int32)
            query_block = lax.dynamic_slice_in_dim(query, start, TOK_DEV, 0)
            keys = lax.dynamic_update_slice_in_dim(keys_cache, lax.dynamic_slice_in_dim(key_new, start, TOK_DEV, 0), start, 0)
            values = lax.dynamic_update_slice_in_dim(values_cache, lax.dynamic_slice_in_dim(value_new, start, TOK_DEV, 0), start, 0)
            scores = jnp.einsum('qhd,khd->hqk', query_block.astype(jnp.float32), keys.astype(jnp.float32)) / math.sqrt(HD)
            prob = jax.nn.softmax(scores, axis=-1).astype(jnp.bfloat16)
            mixed = jnp.einsum('hqk,khd->qhd', prob.astype(jnp.float32), values.astype(jnp.float32))
            return mixed.astype(jnp.bfloat16)
        attended = lax.map(block, jnp.arange(N_PATCH, dtype=jnp.int32)).reshape(TOKENS, HEADS * HD)
        hidden = jax.nn.gelu(jnp.dot(h, w_in, preferred_element_type=jnp.float32), approximate=True).astype(jnp.bfloat16)
        velocity = jnp.zeros((TOKENS, D), jnp.float32)
        for rank in range(N_HEAD):
            term = jnp.dot(attended[:, rank * group:(rank + 1) * group], w_attn[rank * group:(rank + 1) * group], preferred_element_type=jnp.float32)
            term = term + jnp.dot(hidden[:, rank * ffd:(rank + 1) * ffd], w_out[rank * ffd:(rank + 1) * ffd], preferred_element_type=jnp.float32)
            velocity = velocity + lax.optimization_barrier(term.astype(jnp.bfloat16)).astype(jnp.float32)
        if step < STEPS - 1:
            delta_keys = (key_new.astype(jnp.float32) - keys_cache.astype(jnp.float32)).astype(jnp.bfloat16)
            delta_values = (value_new.astype(jnp.float32) - values_cache.astype(jnp.float32)).astype(jnp.bfloat16)
            keys_cache = (keys_cache.astype(jnp.float32) + lax.optimization_barrier(delta_keys).astype(jnp.float32)).astype(jnp.bfloat16)
            values_cache = (values_cache.astype(jnp.float32) + lax.optimization_barrier(delta_values).astype(jnp.float32)).astype(jnp.bfloat16)
        x = x + (level_b - level_a) * velocity
    return x
```

```python
import math

import jax
import jax.numpy as jnp
from jax import lax
from jax.experimental import pallas as pl
from jax.experimental.pallas import tpu as pltpu
from jax.sharding import PartitionSpec as P

MESH = pl.DeviceIdType.MESH
F32 = jnp.float32
BF16 = jnp.bfloat16
SCHED = 1000
STEPS = 3
Z = 16
CHIPS = 16
TOK = 128
D = 3072
HALF = D // 2
HD = 128
ROWS = 96
KEYS = 4096
CHUNK = 512
NT = (((1,), (1,)), ((), ()))


def sigma(unit_index):
    unit = 1.0 - unit_index / SCHED
    return 3.0 * unit / (1.0 + 2.0 * unit)


def kernel(
    times, state, mod_w, w_qkv, w_in, w_attn, w_out, q_gain, k_gain, cache_k, cache_v,
    out,
    wq, wi, wo, kv, hland, rland, tsend, hb, og, scores, xs, xl, fs, fl, xt, mw, modp, xp, gains,
    cache_s, cache_r, swap_s, swap_r, ring_s, ring_r, pair_s, pair_r,
    kring_s, kring_r, kpair_s, kpair_r, x_s, x_r, ag_s, ag_r, rs_s, rs_r, f_s, f_r, local,
):
    patch = lax.axis_index("patch")
    head = lax.axis_index("head")
    yl, z = lax.div(patch, Z), lax.rem(patch, Z)
    yh, x, c = lax.div(head, 8), lax.rem(lax.div(head, 2), 4), lax.rem(head, 2)
    y = yh * 2 + yl
    me = y * 4 + x
    own = c * Z + z
    natural = c == yl

    def dev(yy, xx, cc, zz):
        return (lax.rem(yy, 2) * Z + zz, lax.div(yy, 2) * 8 + xx * 2 + cc)

    def chip_at(o):
        return lax.rem(y + lax.div(o, 4), 4), lax.rem(x + lax.rem(o, 4), 4)

    def chip_from(o):
        return lax.rem(y + 4 - lax.div(o, 4), 4), lax.rem(x + 4 - lax.rem(o, 4), 4)

    def remote(src, dst, send, recv, device):
        return pltpu.make_async_remote_copy(
            src_ref=src, dst_ref=dst, send_sem=send, recv_sem=recv, device_id=device, device_id_type=MESH
        )

    partner = dev(y, x, 1 - c, z)
    z_next = (dev(y, x, c, lax.rem(z + 1, Z)), dev(y, x, c, lax.rem(z + Z - 1, Z)))
    twin = dev(yh * 2 + c, x, yl, z)

    barrier = pltpu.get_barrier_semaphore()

    def greet(device):
        pl.semaphore_signal(barrier, inc=1, device_id=device, device_id_type=MESH)

    def greet_chip(o, carry):
        yy, xx = chip_at(o)
        greet(dev(yy, xx, c, z))
        greet(dev(yy, xx, 1 - c, z))
        return carry

    greet(z_next[0])
    greet(z_next[1])
    greet(partner)
    lax.fori_loop(1, CHIPS, greet_chip, 0)

    weights = (wq, wi, wo)

    def slab(j, zz, part=None):
        start, size = (c * Z + zz) * ROWS, ROWS
        if part is not None:
            start, size = start + part * (ROWS // 2), ROWS // 2
        return weights[j].at[pl.ds(pl.multiple_of(start, 16), size), :]

    def shard_parts():
        base = pl.ds(pl.multiple_of(own * ROWS, 16), ROWS)
        swapped = pl.ds(pl.multiple_of((yl * Z + z) * ROWS, 16), ROWS)
        return (
            (w_qkv, wq.at[base, :], wq.at[swapped, :]),
            (w_in, wi.at[base, :], wi.at[swapped, :]),
            (w_attn, wo.at[base, 0:HD], wo.at[swapped, 0:HD]),
            (w_out, wo.at[base, HD:512], wo.at[swapped, HD:512]),
        )

    def caches():
        return (
            (cache_k, kv.at[0, 0]),
            (cache_v, kv.at[0, 1]),
            (q_gain, gains.at[0]),
            (k_gain, gains.at[1]),
        )

    pl.semaphore_wait(barrier, 33)

    for i, (src, here, there) in enumerate(shard_parts()):
        @pl.when(natural)
        def _():
            pltpu.make_async_copy(src, here, swap_r.at[i]).start()

        @pl.when(jnp.logical_not(natural))
        def _():
            remote(src, there, swap_s.at[i], swap_r.at[i], twin).start()

    @pl.when(natural)
    def _():
        for i, (src, dst) in enumerate(caches()):
            pltpu.make_async_copy(src, dst, local.at[i]).start()
            remote(src, dst, cache_s.at[i], cache_r.at[i], partner).start()

    def wait_own(i):
        src, here, there = shard_parts()[i]
        pltpu.make_async_copy(src, here, swap_r.at[i]).wait()

    def pair_copy(j, zz):
        part = slab(j, zz)
        return remote(part, part, pair_s.at[j, zz], pair_r.at[j, zz], partner)

    def pair_wait(j, zz):
        start = pl.multiple_of(((1 - c) * Z + zz) * ROWS, 16)
        part = weights[j].at[pl.ds(start, ROWS), :]
        remote(part, part, pair_s.at[j, zz], pair_r.at[j, zz], partner).wait_recv()

    def ring_copy(j, d, k, zz, part=None):
        block = slab(j, zz, part)
        return remote(block, block, ring_s.at[j, d, k], ring_r.at[j, d, k], z_next[d])

    def source(d, k):
        return lax.rem(z + Z - k, Z) if d == 0 else lax.rem(z + k, Z)

    def ring_start():
        for j in range(3):
            wait_own(j)
            if j == 2:
                wait_own(3)
            for d in range(2):
                ring_copy(j, d, 0, z).start()
            pair_copy(j, z).start()

    def ring_hop(k, last=False):
        for j in range(3):
            for d in range(2):
                zz = source(d, k)
                ring_copy(j, d, k - 1, zz).wait_recv()
                ring_copy(j, d, k, zz, d if last else None).start()
                pair_copy(j, zz).start()

    def ring_end():
        zz = source(0, 8)
        for j in range(3):
            for d in range(2):
                ring_copy(j, d, 7, zz, d).wait_recv()
            pair_copy(j, zz).start()

    ring_start()

    row = lax.broadcasted_iota(jnp.int32, (8, HD), 0)
    lane = lax.broadcasted_iota(jnp.int32, (8, HD), 1)
    stepped = lax.rem(row, 3)
    when = jnp.zeros((8, HD), F32)
    for s in range(STEPS):
        when = jnp.where(stepped == s, times[s].astype(F32), when)
    freq = jnp.exp(-math.log(10000.0) * lane.astype(F32) / HD)
    angle = 1000.0 * sigma(when) * freq
    emb = jnp.concatenate([jnp.cos(angle), jnp.sin(angle)], axis=1).astype(BF16)
    place = pl.ds(pl.multiple_of(c * 64, 64), 192)
    mw[...] = jnp.zeros_like(mw)
    xt[...] = jnp.zeros_like(xt)
    for j in range(2):
        mw[j, place, :] = mod_w[j]
    xt[place, :] = state[...]
    mods = [lax.dot_general(emb, mw[j], NT, preferred_element_type=F32) for j in range(2)]
    row2 = lax.broadcasted_iota(jnp.int32, (8, 256), 0)
    mod_rows = jnp.where(row2 < 3, mods[0], mods[1])
    rows_here = xt[...].T
    for q in range(CHIPS):
        xs[q, 0:8] = rows_here[8 * q : 8 * q + 8]
        xs[q, 8:16] = mod_rows

    def x_copy(q, device):
        return remote(xs.at[q], xl.at[head], x_s.at[q], x_r.at[head], device)

    @pl.when(natural)
    def _():
        pltpu.make_async_copy(xs.at[me], xl.at[head], x_r.at[head]).start()

    @pl.when(jnp.logical_not(natural))
    def _():
        x_copy(me, partner).start()

    def x_start(o, carry):
        yy, xx = chip_at(o)
        x_copy(yy * 4 + xx, dev(yy, xx, yl, z)).start()
        return carry

    lax.fori_loop(1, CHIPS, x_start, 0)

    def loop_hops(lo, hi):
        def body(k, carry):
            ring_hop(k)
            return carry

        lax.fori_loop(lo, hi, body, 0)

    loop_hops(1, 3)

    def x_wait(r, carry):
        remote(xs.at[0], xl.at[r], x_s.at[0], x_r.at[r], partner).wait_recv()
        return carry

    lax.fori_loop(0, CHIPS, x_wait, 0)
    for k in range(8):
        a, b = xl[2 * k], xl[2 * k + 1]
        group = jnp.concatenate([a[:, :HD], a[:, HD:] + b[:, :HD], b[:, HD:]], axis=1)
        rows, cols = slice(8 * (k // 4), 8 * (k // 4) + 8), slice(384 * (k % 4), 384 * (k % 4) + 384)
        xp[rows, cols] = group[0:8]
        for i in range(6):
            modp[i, rows, cols] = jnp.broadcast_to(group[8 + i : 9 + i], (8, 384))

    def fold(sums):
        total = (sums[0:8] + sums[8:16]) * (1.0 / D)
        return jnp.concatenate([total, total], axis=0)

    my_slot = pl.ds(pl.multiple_of(me * 16, 16), 16)

    def slot(yy, xx):
        return pl.ds(pl.multiple_of((yy * 4 + xx) * 16, 16), 16)

    def ag_start(s):
        rows = xp[...]
        delta = rows - fold(jnp.sum(rows, axis=1, keepdims=True))
        var = fold(jnp.sum(delta * delta, axis=1, keepdims=True))
        h = delta * lax.rsqrt(var + 1e-06) * (1.0 + modp[s]) + modp[3 + s]
        hland[s, my_slot, :] = h.astype(BF16)

        def body(o, carry):
            yy, xx = chip_at(o)
            block = hland.at[s, my_slot, :]
            remote(block, block, ag_s.at[s, o], ag_r.at[s, o], dev(yy, xx, c, z)).start()
            return carry

        lax.fori_loop(1, CHIPS, body, 0)

    def ag_wait(s, lo=1, hi=CHIPS):
        def body(o, carry):
            yy, xx = chip_from(o)
            block = hland.at[s, slot(yy, xx), :]
            remote(block, block, ag_s.at[s, o], ag_r.at[s, o], partner).wait_recv()
            return carry

        lax.fori_loop(lo, hi, body, 0)

    def unpack(s):
        for m in range(8):
            block = hland[s, 32 * m : 32 * m + 32, :].astype(F32)
            rows = slice(16 * m, 16 * m + 16)
            hb[rows, 0:HALF] = jnp.concatenate([block[0:8], block[16:24]], axis=0).astype(BF16)
            hb[rows, HALF:D] = jnp.concatenate([block[8:16], block[24:32]], axis=0).astype(BF16)

    ag_start(0)
    loop_hops(3, 7)
    ag_wait(0)
    unpack(0)
    ring_hop(7, last=True)
    ring_end()

    def pair_loop(zz, carry):
        for j in range(3):
            pair_wait(j, zz)
        return carry

    lax.fori_loop(0, Z, pair_loop, 0)

    @pl.when(natural)
    def _():
        for i, (src, dst) in enumerate(caches()):
            pltpu.make_async_copy(src, dst, local.at[i]).wait()
            remote(src, dst, cache_s.at[i], cache_r.at[i], partner).wait_send()

    @pl.when(jnp.logical_not(natural))
    def _():
        for i, (src, dst) in enumerate(caches()):
            remote(src, dst, cache_s.at[i], cache_r.at[i], partner).wait_recv()

    def kv_block(s, cc, zz, part=None):
        start, size = (cc * Z + zz) * TOK, TOK
        if part is not None:
            start, size = start + part * (TOK // 2), TOK // 2
        return kv.at[s + 1, :, pl.ds(pl.multiple_of(start, 16), size), :]

    def kring_copy(s, d, k, zz, part=None):
        block = kv_block(s, c, zz, part)
        return remote(block, block, kring_s.at[s, d, k], kring_r.at[s, d, k], z_next[d])

    def kpair_copy(s, zz):
        block = kv_block(s, c, zz)
        return remote(block, block, kpair_s.at[s, zz], kpair_r.at[s, zz], partner)

    def kv_start(s):
        for d in range(2):
            kring_copy(s, d, 0, z).start()
        kpair_copy(s, z).start()

    def kv_hop(s, k):
        if s >= STEPS - 1:
            return
        if k < 8:
            for d in range(2):
                zz = source(d, k)
                kring_copy(s, d, k - 1, zz).wait_recv()
                kring_copy(s, d, k, zz, d if k == 7 else None).start()
                kpair_copy(s, zz).start()
        else:
            zz = source(0, 8)
            for d in range(2):
                kring_copy(s, d, 7, zz, d).wait_recv()
            kpair_copy(s, zz).start()

    def kv_wait(s):
        def body(zz, carry):
            block = kv_block(s, 1 - c, zz)
            remote(block, block, kpair_s.at[s, zz], kpair_r.at[s, zz], partner).wait_recv()
            return carry

        lax.fori_loop(0, Z, body, 0)

    def kv_sent(s):
        def body(k, carry):
            for d in range(2):
                kring_copy(s, d, k, z).wait_send()
            return carry

        lax.fori_loop(0, 7, body, 0)
        for d in range(2):
            kring_copy(s, d, 7, z, d).wait_send()

        def pairs(zz, carry):
            kpair_copy(s, zz).wait_send()
            return carry

        lax.fori_loop(0, Z, pairs, 0)

    def rms(values, gain):
        return values * lax.rsqrt(jnp.mean(values * values, axis=1, keepdims=True) + 1e-06) * gain

    own_rows = pl.ds(pl.multiple_of(own * TOK, 16), TOK)

    for s in range(STEPS):
        qkv = jnp.dot(hb[...], wq[...], preferred_element_type=F32)
        query = rms(qkv[:, 0:HD], gains[0]).astype(BF16)
        fresh = (rms(qkv[:, HD : 2 * HD], gains[1]).astype(BF16), qkv[:, 2 * HD :].astype(BF16))
        if s > 0:
            kv_sent(s - 1)
        for i in range(2):
            old = kv[s, i, own_rows, :].astype(F32)
            if s < STEPS - 1:
                change = (fresh[i].astype(F32) - old).astype(BF16)
                kv[s + 1, i, own_rows, :] = (old + change.astype(F32)).astype(BF16)
            kv[s, i, own_rows, :] = fresh[i]
        if s < STEPS - 1:
            kv_start(s)
        top = jnp.full((TOK, 1), -jnp.inf, F32)
        for j in range(KEYS // CHUNK):
            cols = slice(CHUNK * j, CHUNK * j + CHUNK)
            score = lax.dot_general(query, kv[s, 0, cols, :], NT, preferred_element_type=F32)
            score = score * (1.0 / math.sqrt(HD))
            scores[:, cols] = score
            top = jnp.maximum(top, jnp.max(score, axis=1, keepdims=True))
        mass = jnp.zeros((TOK, 1), F32)
        mixed = jnp.zeros((TOK, HD), F32)
        for j in range(KEYS // CHUNK):
            cols = slice(CHUNK * j, CHUNK * j + CHUNK)
            weight = jnp.exp(scores[:, cols] - top)
            mass = mass + jnp.sum(weight, axis=1, keepdims=True)
            mixed = mixed + jnp.dot(weight.astype(BF16), kv[s, 1, cols, :], preferred_element_type=F32)
        og[:, 0:HD] = (mixed / mass).astype(BF16)
        kv_hop(s, 1)
        og[:, HD:512] = jax.nn.gelu(
            jnp.dot(hb[...], wi[...], preferred_element_type=F32), approximate=True
        ).astype(BF16)
        kv_hop(s, 2)
        if s > 0:
            def rs_sent(o, carry):
                block = tsend.at[my_slot, :]
                remote(block, block, rs_s.at[s - 1, o], rs_r.at[s - 1, o], partner).wait_send()
                return carry

            lax.fori_loop(1, CHIPS, rs_sent, 0)
        for n in range(4):
            cols = slice(384 * n, 384 * n + 384)
            upper = slice(HALF + 384 * n, HALF + 384 * n + 384)
            low = lax.dot_general(og[...], wo[cols, :], NT, preferred_element_type=F32)
            high = lax.dot_general(og[...], wo[upper, :], NT, preferred_element_type=F32)
            both = jnp.concatenate([low.reshape(CHIPS, 8, 384), high.reshape(CHIPS, 8, 384)], axis=1)
            tsend[:, cols] = both.reshape(CHIPS * 16, 384).astype(BF16)
        rland[s, my_slot, :] = tsend[my_slot, :]

        def rs_start(o, carry):
            yy, xx = chip_at(o)
            remote(
                tsend.at[slot(yy, xx), :], rland.at[s, my_slot, :], rs_s.at[s, o], rs_r.at[s, o],
                dev(yy, xx, c, z),
            ).start()
            return carry

        lax.fori_loop(1, CHIPS, rs_start, 0)
        kv_hop(s, 3)

        def rs_wait(o, carry):
            yy, xx = chip_from(o)
            remote(
                tsend.at[my_slot, :], rland.at[s, slot(yy, xx), :], rs_s.at[s, o], rs_r.at[s, o], partner
            ).wait_recv()
            return carry

        lax.fori_loop(1, 8, rs_wait, 0)
        kv_hop(s, 4)
        lax.fori_loop(8, CHIPS, rs_wait, 0)
        total = jnp.zeros((16, HALF), F32)
        for q in range(CHIPS):
            total = total + rland[s, 16 * q : 16 * q + 16, :].astype(F32)
        level = [sigma(jnp.full((16, HD), times[s + i].astype(F32))) for i in range(2)]
        gap = (level[1] - level[0])[:, 0:1]
        xp[...] = xp[...] + gap * total
        if s < STEPS - 1:
            ag_start(s + 1)
            kv_hop(s, 5)
            ag_wait(s + 1, 1, 6)
            kv_hop(s, 6)
            ag_wait(s + 1, 6, 11)
            kv_hop(s, 7)
            ag_wait(s + 1, 11, CHIPS)
            unpack(s + 1)
            kv_hop(s, 8)
            kv_wait(s)

    for r in range(CHIPS):
        k = r // 2
        first = 384 * (k % 4) + HD * (r % 2)
        fs[r] = xp[8 * (k // 4) : 8 * (k // 4) + 8, first : first + 256]

    def f_copy(r):
        rows = pl.ds(pl.multiple_of(me * 8, 8), 8)
        return remote(fs.at[r], fl.at[rows, :], f_s.at[r], f_r.at[me], (c * Z + z, r))

    def f_self():
        rows = pl.ds(pl.multiple_of(me * 8, 8), 8)
        return pltpu.make_async_copy(fs.at[head], fl.at[rows, :], f_r.at[me])

    def f_start(o, carry):
        r = lax.rem(head + o, CHIPS)
        f_copy(r).start()
        return carry

    lax.fori_loop(1, CHIPS, f_start, 0)

    @pl.when(natural)
    def _():
        f_self().start()

    @pl.when(jnp.logical_not(natural))
    def _():
        f_copy(head).start()

    def f_wait(q, carry):
        rows = pl.ds(pl.multiple_of(q * 8, 8), 8)
        remote(fs.at[0], fl.at[rows, :], f_s.at[0], f_r.at[q], partner).wait_recv()
        return carry

    lax.fori_loop(0, CHIPS, f_wait, 0)
    xt[...] = fl[...].T
    out[...] = xt[place, :]

    def all_sent(o, carry):
        remote(xs.at[0], xl.at[0], x_s.at[lax.rem(me + o, CHIPS)], x_r.at[0], partner).wait_send()
        f_copy(lax.rem(head + o, CHIPS)).wait_send()
        for s in range(STEPS):
            block = hland.at[s, my_slot, :]
            remote(block, block, ag_s.at[s, o], ag_r.at[s, o], partner).wait_send()
        block = tsend.at[my_slot, :]
        remote(block, block, rs_s.at[STEPS - 1, o], rs_r.at[STEPS - 1, o], partner).wait_send()
        return carry

    lax.fori_loop(1, CHIPS, all_sent, 0)

    @pl.when(jnp.logical_not(natural))
    def _():
        x_copy(me, partner).wait_send()
        f_copy(head).wait_send()
        for i, (src, here, there) in enumerate(shard_parts()):
            remote(src, there, swap_s.at[i], swap_r.at[i], twin).wait_send()

    def ring_sent(k, carry):
        for j in range(3):
            for d in range(2):
                ring_copy(j, d, k, z).wait_send()
        return carry

    lax.fori_loop(0, 7, ring_sent, 0)
    for j in range(3):
        for d in range(2):
            ring_copy(j, d, 7, z, d).wait_send()

    def pair_sent(zz, carry):
        for j in range(3):
            pair_copy(j, zz).wait_send()
        return carry

    lax.fori_loop(0, Z, pair_sent, 0)


def on_device(
    state, mod_weight, w_qkv, q_gain, k_gain, w_in, w_attn, w_out, cache_keys, cache_values, timesteps
):
    vmem = pl.BlockSpec(memory_space=pltpu.VMEM)
    hbm = pl.BlockSpec(memory_space=pl.ANY)
    smem = pl.BlockSpec(memory_space=pltpu.SMEM)
    dma = pltpu.SemaphoreType.DMA
    result = pl.pallas_call(
        kernel,
        out_shape=jax.ShapeDtypeStruct((192, TOK), F32),
        in_specs=[smem, vmem, vmem, hbm, hbm, hbm, hbm, hbm, hbm, hbm, hbm],
        out_specs=vmem,
        scratch_shapes=[
            pltpu.VMEM((D, 384), BF16),
            pltpu.VMEM((D, 384), BF16),
            pltpu.VMEM((D, 512), BF16),
            pltpu.VMEM((STEPS, 2, KEYS, HD), BF16),
            pltpu.VMEM((STEPS, CHIPS * 16, HALF), BF16),
            pltpu.VMEM((STEPS, CHIPS * 16, HALF), BF16),
            pltpu.VMEM((CHIPS * 16, HALF), BF16),
            pltpu.VMEM((TOK, D), BF16),
            pltpu.VMEM((TOK, 512), BF16),
            pltpu.VMEM((TOK, KEYS), F32),
            pltpu.VMEM((CHIPS, 16, 256), F32),
            pltpu.VMEM((CHIPS, 16, 256), F32),
            pltpu.VMEM((CHIPS, 8, 256), F32),
            pltpu.VMEM((TOK, 256), F32),
            pltpu.VMEM((256, TOK), F32),
            pltpu.VMEM((2, 256, 256), BF16),
            pltpu.VMEM((6, 16, HALF), F32),
            pltpu.VMEM((16, HALF), F32),
            pltpu.VMEM((2, 1, HD), F32),
            dma((4,)), dma((4,)), dma((4,)), dma((4,)),
            dma((3, 2, 8)), dma((3, 2, 8)), dma((3, Z)), dma((3, Z)),
            dma((2, 2, 8)), dma((2, 2, 8)), dma((2, Z)), dma((2, Z)),
            dma((CHIPS,)), dma((CHIPS,)),
            dma((STEPS, CHIPS)), dma((STEPS, CHIPS)), dma((STEPS, CHIPS)), dma((STEPS, CHIPS)),
            dma((CHIPS,)), dma((CHIPS,)), dma((4,)),
        ],
        compiler_params=pltpu.CompilerParams(
            collective_id=0, has_side_effects=True, vmem_limit_bytes=48 * 1024 * 1024
        ),
    )(
        timesteps,
        state.T,
        jnp.transpose(mod_weight, (1, 2, 0)),
        w_qkv.reshape(ROWS, 384),
        w_in,
        w_attn.T,
        w_out.T,
        q_gain,
        k_gain,
        cache_keys.reshape(KEYS, HD),
        cache_values.reshape(KEYS, HD),
    )
    return result.T


def solution(mesh):
    in_specs = (
        P("patch", "head"),
        P(None, None, "head"),
        P("patch", "head", None),
        P("head", None),
        P("head", None),
        P("patch", "head"),
        P("head", "patch"),
        P("head", "patch"),
        P(None, "head", None),
        P(None, "head", None),
        P(),
    )
    return jax.shard_map(
        on_device, mesh=mesh, in_specs=in_specs, out_specs=P("patch", "head"), check_vma=False
    )
```

```python
import math

import jax
import jax.numpy as jnp
from jax import lax
from jax.experimental import pallas as pl
from jax.experimental.pallas import tpu as pltpu
from jax.sharding import PartitionSpec as P

MESH = pl.DeviceIdType.MESH
F32 = jnp.float32
BF16 = jnp.bfloat16
SCHED = 1000
STEPS = 3
Z = 16
CHIPS = 16
TOK = 128
D = 3072
HALF = D // 2
PART = HALF // 2
HD = 128
ROWS = 96
KEYS = 4096
CHUNK = 512
NT = (((1,), (1,)), ((), ()))


def sigma(unit_index):
    unit = 1.0 - unit_index / SCHED
    return 3.0 * unit / (1.0 + 2.0 * unit)


def kernel(
    times, state, mod_w, w_qkv, w_in, w_attn, w_out, q_gain, k_gain, cache_k, cache_v,
    out,
    wq, wi, wo, kv, hland, r1, r2, tsend, p2, hb, og, scores, xs, xl, fs, fl, xt, mw, modp, xp, gains,
    cache_s, cache_r, swap_s, swap_r, ring_s, ring_r, pair_s, pair_r,
    kring_s, kring_r, kpair_s, kpair_r, x_s, x_r, ag1_s, ag1_r, ag2_s, ag2_r,
    rs1_s, rs1_r, rs2_s, rs2_r, f_s, f_r, local,
):
    patch = lax.axis_index("patch")
    head = lax.axis_index("head")
    yl, z = lax.div(patch, Z), lax.rem(patch, Z)
    yh, x, c = lax.div(head, 8), lax.rem(lax.div(head, 2), 4), lax.rem(head, 2)
    y = yh * 2 + yl
    me = y * 4 + x
    own = c * Z + z
    natural = c == yl

    def dev(yy, xx, cc, zz):
        return (lax.rem(yy, 2) * Z + zz, lax.div(yy, 2) * 8 + xx * 2 + cc)

    def chip_at(o):
        return lax.rem(y + lax.div(o, 4), 4), lax.rem(x + lax.rem(o, 4), 4)

    def remote(src, dst, send, recv, device):
        return pltpu.make_async_remote_copy(
            src_ref=src, dst_ref=dst, send_sem=send, recv_sem=recv, device_id=device, device_id_type=MESH
        )

    partner = dev(y, x, 1 - c, z)
    z_next = (dev(y, x, c, lax.rem(z + 1, Z)), dev(y, x, c, lax.rem(z + Z - 1, Z)))
    z_far = (dev(y, x, c, lax.rem(z + 2, Z)), dev(y, x, c, lax.rem(z + Z - 2, Z)))
    twin = dev(yh * 2 + c, x, yl, z)

    barrier = pltpu.get_barrier_semaphore()

    def greet(device):
        pl.semaphore_signal(barrier, inc=1, device_id=device, device_id_type=MESH)

    def greet_chip(o, carry):
        yy, xx = chip_at(o)
        greet(dev(yy, xx, c, z))
        greet(dev(yy, xx, 1 - c, z))
        return carry

    for device in z_next + z_far:
        greet(device)
    greet(partner)
    lax.fori_loop(1, CHIPS, greet_chip, 0)

    weights = (wq, wi, wo)

    def slab(j, zz, part=None):
        start, size = (c * Z + zz) * ROWS, ROWS
        if part is not None:
            start, size = start + part * (ROWS // 2), ROWS // 2
        return weights[j].at[pl.ds(pl.multiple_of(start, 16), size), :]

    def shard_parts():
        base = pl.ds(pl.multiple_of(own * ROWS, 16), ROWS)
        swapped = pl.ds(pl.multiple_of((yl * Z + z) * ROWS, 16), ROWS)
        return (
            (w_qkv, wq.at[base, :], wq.at[swapped, :]),
            (w_in, wi.at[base, :], wi.at[swapped, :]),
            (w_attn, wo.at[base, 0:HD], wo.at[swapped, 0:HD]),
            (w_out, wo.at[base, HD:512], wo.at[swapped, HD:512]),
        )

    def caches():
        return (
            (cache_k, kv.at[0, 0]),
            (cache_v, kv.at[0, 1]),
            (q_gain, gains.at[0]),
            (k_gain, gains.at[1]),
        )


    @pl.when(natural)
    def _():
        for i, (src, here, there) in enumerate(shard_parts()):
            pltpu.make_async_copy(src, here, swap_r.at[i]).start()
        for i, (src, dst) in enumerate(caches()):
            pltpu.make_async_copy(src, dst, local.at[i]).start()

    row = lax.broadcasted_iota(jnp.int32, (8, HD), 0)
    lane = lax.broadcasted_iota(jnp.int32, (8, HD), 1)
    stepped = lax.rem(row, 3)
    when = jnp.zeros((8, HD), F32)
    for s in range(STEPS):
        when = jnp.where(stepped == s, times[s].astype(F32), when)
    freq = jnp.exp(-math.log(10000.0) * lane.astype(F32) / HD)
    angle = 1000.0 * sigma(when) * freq
    emb = jnp.concatenate([jnp.cos(angle), jnp.sin(angle)], axis=1).astype(BF16)
    place = pl.ds(pl.multiple_of(c * 64, 64), 192)
    mw[...] = jnp.zeros_like(mw)
    xt[...] = jnp.zeros_like(xt)
    for j in range(2):
        mw[j, place, :] = mod_w[j]
    xt[place, :] = state[...]
    mods = [lax.dot_general(emb, mw[j], NT, preferred_element_type=F32) for j in range(2)]
    row2 = lax.broadcasted_iota(jnp.int32, (8, 256), 0)
    mod_rows = jnp.where(row2 < 3, mods[0], mods[1])
    rows_here = xt[...].T
    for q in range(CHIPS):
        xs[q, 0:8] = rows_here[8 * q : 8 * q + 8]
        xs[q, 8:16] = mod_rows

    pl.semaphore_wait(barrier, 35)

    @pl.when(jnp.logical_not(natural))
    def _():
        for i, (src, here, there) in enumerate(shard_parts()):
            remote(src, there, swap_s.at[i], swap_r.at[i], twin).start()

    @pl.when(natural)
    def _():
        for i, (src, dst) in enumerate(caches()):
            remote(src, dst, cache_s.at[i], cache_r.at[i], partner).start()

    def wait_own(i):
        src, here, there = shard_parts()[i]
        pltpu.make_async_copy(src, here, swap_r.at[i]).wait()

    def pair_copy(j, zz):
        part = slab(j, zz)
        return remote(part, part, pair_s.at[j, zz], pair_r.at[j, zz], partner)

    def pair_wait(j, zz):
        start = pl.multiple_of(((1 - c) * Z + zz) * ROWS, 16)
        part = weights[j].at[pl.ds(start, ROWS), :]
        remote(part, part, pair_s.at[j, zz], pair_r.at[j, zz], partner).wait_recv()

    def ring_copy(j, d, k, zz, part=None):
        block = slab(j, zz, part)
        return remote(block, block, ring_s.at[j, d, k], ring_r.at[j, d, k], z_next[d])

    def source(d, k):
        return lax.rem(z + Z - k, Z) if d == 0 else lax.rem(z + k, Z)

    def ring_start():
        for j in range(3):
            wait_own(j)
            if j == 2:
                wait_own(3)
            for d in range(2):
                ring_copy(j, d, 0, z).start()
            pair_copy(j, z).start()

    def ring_hop(k, last=False):
        for j in range(3):
            for d in range(2):
                zz = source(d, k)
                ring_copy(j, d, k - 1, zz).wait_recv()
                ring_copy(j, d, k, zz, d if last else None).start()
                pair_copy(j, zz).start()

    def ring_end(j):
        zz = source(0, 8)
        for d in range(2):
            ring_copy(j, d, 7, zz, d).wait_recv()
        pair_copy(j, zz).start()

    def pair_all(j):
        def body(zz, carry):
            pair_wait(j, zz)
            return carry

        lax.fori_loop(0, Z, body, 0)

    ring_start()

    def x_copy(q, device):
        return remote(xs.at[q], xl.at[head], x_s.at[q], x_r.at[head], device)

    @pl.when(natural)
    def _():
        pltpu.make_async_copy(xs.at[me], xl.at[head], x_r.at[head]).start()

    @pl.when(jnp.logical_not(natural))
    def _():
        x_copy(me, partner).start()

    def x_start(o, carry):
        yy, xx = chip_at(o)
        x_copy(yy * 4 + xx, dev(yy, xx, yl, z)).start()
        return carry

    lax.fori_loop(1, CHIPS, x_start, 0)

    def loop_hops(lo, hi):
        def body(k, carry):
            ring_hop(k)
            return carry

        lax.fori_loop(lo, hi, body, 0)

    loop_hops(1, 3)

    def x_wait(r, carry):
        remote(xs.at[0], xl.at[r], x_s.at[0], x_r.at[r], partner).wait_recv()
        return carry

    lax.fori_loop(0, CHIPS, x_wait, 0)
    for k in range(8):
        a, b = xl[2 * k], xl[2 * k + 1]
        group = jnp.concatenate([a[:, :HD], a[:, HD:] + b[:, :HD], b[:, HD:]], axis=1)
        rows, cols = slice(8 * (k // 4), 8 * (k // 4) + 8), slice(384 * (k % 4), 384 * (k % 4) + 384)
        xp[rows, cols] = group[0:8]
        for i in range(6):
            modp[i, rows, cols] = jnp.broadcast_to(group[8 + i : 9 + i], (8, 384))

    def fold(sums):
        total = (sums[0:8] + sums[8:16]) * (1.0 / D)
        return jnp.concatenate([total, total], axis=0)

    def turn(i, d):
        return lax.rem(i + d, 4)

    def slot(yy, xx):
        return pl.ds(pl.multiple_of((yy * 4 + xx) * 16, 16), 16)

    def line(half, d):
        return dev(y, turn(x, d), c, z) if half == 0 else dev(turn(y, d), x, c, z)

    def origin(half, d1, d2=0):
        dy, dx = (d2, d1) if half == 0 else (d1, d2)
        return slot(turn(y, 4 - dy), turn(x, 4 - dx))

    def ag1(s, half, d, rows):
        block = hland.at[s, half, rows, :]
        return remote(block, block, ag1_s.at[s, half, d], ag1_r.at[s, half, d], line(half, d))

    def ag2(s, half, d1, d2, rows):
        block = hland.at[s, half, rows, :]
        i = d1 * 4 + d2
        return remote(block, block, ag2_s.at[s, half, i], ag2_r.at[s, half, i], line(1 - half, d2))

    def ag_start(s):
        rows = xp[...]
        delta = rows - fold(jnp.sum(rows, axis=1, keepdims=True))
        var = fold(jnp.sum(delta * delta, axis=1, keepdims=True))
        h = (delta * lax.rsqrt(var + 1e-06) * (1.0 + modp[s]) + modp[3 + s]).astype(BF16)
        mine = slot(y, x)
        for half in range(2):
            hland[s, half, mine, :] = h[:, half * PART : half * PART + PART]
        for d in (1, 3, 2):
            for half in range(2):
                ag1(s, half, d, mine).start()
        for d in (1, 3, 2):
            for half in range(2):
                ag2(s, half, 0, d, mine).start()

    def ag_forward(s):
        for d in (1, 3, 2):
            for half in range(2):
                rows = origin(half, d)
                ag1(s, half, d, rows).wait_recv()
                for e in (1, 3, 2):
                    ag2(s, half, d, e, rows).start()

    def ag_end(s, half):
        for d in (0, 1, 3, 2):
            for e in (1, 3, 2):
                ag2(s, half, d, e, origin(half, d, e)).wait_recv()

    def ag_sent(s):
        mine = slot(y, x)
        for half in range(2):
            for e in (1, 2, 3):
                ag1(s, half, e, mine).wait_send()
                for d in range(4):
                    ag2(s, half, d, e, mine).wait_send()

    def rs1(s, half, d):
        to = turn(y if half == 0 else x, d)
        block = tsend.at[half, pl.ds(pl.multiple_of(to * 64, 64), 64), :]
        return remote(
            block, r1.at[s, half, d - 1], rs1_s.at[s, half, d], rs1_r.at[s, half, d], line(1 - half, d)
        )

    def rs2(s, half, d):
        to = turn(x if half == 0 else y, d)
        block = p2.at[half, pl.ds(pl.multiple_of(to * 16, 16), 16), :]
        return remote(
            block, r2.at[s, half, d - 1], rs2_s.at[s, half, d], rs2_r.at[s, half, d], line(half, d)
        )

    def rs_middle(s):
        for half in range(2):
            here = pl.ds(pl.multiple_of((y if half == 0 else x) * 64, 64), 64)
            for d in (1, 3, 2):
                rs1(s, half, d).wait_recv()
            part = tsend[half, here, :].astype(F32)
            for d in range(3):
                part = part + r1[s, half, d].astype(F32)
            p2[half] = part.astype(BF16)
            for d in (1, 3, 2):
                rs2(s, half, d).start()

    def rs_end(s):
        parts = []
        for half in range(2):
            here = pl.ds(pl.multiple_of((x if half == 0 else y) * 16, 16), 16)
            part = p2[half, here, :].astype(F32)
            for d in (1, 3, 2):
                rs2(s, half, d).wait_recv()
                part = part + r2[s, half, d - 1].astype(F32)
            parts.append(part)
        return jnp.concatenate(parts, axis=1)

    def unpack(s, half):
        for m in range(8):
            block = hland[s, half, 32 * m : 32 * m + 32, :].astype(F32)
            rows = slice(16 * m, 16 * m + 16)
            low, high = half * PART, HALF + half * PART
            hb[rows, low : low + PART] = jnp.concatenate([block[0:8], block[16:24]], axis=0).astype(BF16)
            hb[rows, high : high + PART] = jnp.concatenate([block[8:16], block[24:32]], axis=0).astype(BF16)

    ag_start(0)
    loop_hops(3, 5)
    ag_forward(0)
    loop_hops(5, 7)
    for half in range(2):
        ag_end(0, half)
        unpack(0, half)
    ring_hop(7, last=True)
    ring_end(0)
    ring_end(1)
    pair_all(0)

    @pl.when(natural)
    def _():
        for i, (src, dst) in enumerate(caches()):
            pltpu.make_async_copy(src, dst, local.at[i]).wait()
            remote(src, dst, cache_s.at[i], cache_r.at[i], partner).wait_send()

    @pl.when(jnp.logical_not(natural))
    def _():
        for i, (src, dst) in enumerate(caches()):
            remote(src, dst, cache_s.at[i], cache_r.at[i], partner).wait_recv()

    def kv_block(s, cc, zz, part=None):
        start, size = (cc * Z + zz) * TOK, TOK
        if part is not None:
            start, size = start + part * (TOK // 2), TOK // 2
        return kv.at[s + 1, :, pl.ds(pl.multiple_of(start, 16), size), :]

    def kring_copy(s, d, k, far, zz, part=None):
        block = kv_block(s, c, zz, part)
        device = z_far[d] if far else z_next[d]
        return remote(block, block, kring_s.at[s, d, k, far], kring_r.at[s, d, k, far], device)

    def kpair_copy(s, zz):
        block = kv_block(s, c, zz)
        return remote(block, block, kpair_s.at[s, zz], kpair_r.at[s, zz], partner)

    def kv_send(s, k):
        for d in range(2):
            kring_copy(s, d, k, 1, source(d, 2 * k), d if k == 3 else None).start()
        for d in range(2):
            kring_copy(s, d, k, 0, source(d, 2 * k)).start()

    def kv_start(s):
        kv_send(s, 0)
        kpair_copy(s, z).start()

    def kv_stage(s, k):
        for d in range(2):
            kring_copy(s, d, k - 1, 1, source(d, 2 * k), d if k == 4 else None).wait_recv()
        if k < 4:
            kv_send(s, k)
            for d in range(2):
                kpair_copy(s, source(d, 2 * k)).start()
        else:
            kpair_copy(s, source(0, 8)).start()
        for d in range(2):
            zz = source(d, 2 * k - 1)
            kring_copy(s, d, k - 1, 0, zz).wait_recv()
            kpair_copy(s, zz).start()

    def kv_wait(s):
        def body(zz, carry):
            block = kv_block(s, 1 - c, zz)
            remote(block, block, kpair_s.at[s, zz], kpair_r.at[s, zz], partner).wait_recv()
            return carry

        lax.fori_loop(0, Z, body, 0)

    def kv_sent_own(s):
        for d in range(2):
            for far in range(2):
                kring_copy(s, d, 0, far, z).wait_send()
        kpair_copy(s, z).wait_send()

    def kv_sent_rest(s):
        for d in range(2):
            for k in range(1, 4):
                kring_copy(s, d, k, 0, z).wait_send()
                kring_copy(s, d, k, 1, z, d if k == 3 else None).wait_send()

        def pairs(o, carry):
            kpair_copy(s, lax.rem(z + o, Z)).wait_send()
            return carry

        lax.fori_loop(1, Z, pairs, 0)

    def rms(values, gain):
        return values * lax.rsqrt(jnp.mean(values * values, axis=1, keepdims=True) + 1e-06) * gain

    own_rows = pl.ds(pl.multiple_of(own * TOK, 16), TOK)

    for s in range(STEPS):
        qkv = jnp.dot(hb[...], wq[...], preferred_element_type=F32)
        query = rms(qkv[:, 0:HD], gains[0]).astype(BF16)
        fresh = (rms(qkv[:, HD : 2 * HD], gains[1]).astype(BF16), qkv[:, 2 * HD :].astype(BF16))
        if s > 0:
            kv_sent_own(s - 1)
        for i in range(2):
            old = kv[s, i, own_rows, :].astype(F32)
            if s < STEPS - 1:
                change = (fresh[i].astype(F32) - old).astype(BF16)
                kv[s + 1, i, own_rows, :] = (old + change.astype(F32)).astype(BF16)
            kv[s, i, own_rows, :] = fresh[i]
        if s < STEPS - 1:
            kv_start(s)
        if s == 0:
            pair_all(1)
        og[:, HD:512] = jax.nn.gelu(
            jnp.dot(hb[...], wi[...], preferred_element_type=F32), approximate=True
        ).astype(BF16)
        if s == 0:
            ring_end(2)
        else:
            kv_stage(s - 1, 4)
            kv_wait(s - 1)
        top = jnp.full((TOK, 1), -jnp.inf, F32)
        for j in range(KEYS // CHUNK):
            cols = slice(CHUNK * j, CHUNK * j + CHUNK)
            score = lax.dot_general(query, kv[s, 0, cols, :], NT, preferred_element_type=F32)
            score = score * (1.0 / math.sqrt(HD))
            scores[:, cols] = score
            top = jnp.maximum(top, jnp.max(score, axis=1, keepdims=True))
        mass = jnp.zeros((TOK, 1), F32)
        mixed = jnp.zeros((TOK, HD), F32)
        for j in range(KEYS // CHUNK):
            cols = slice(CHUNK * j, CHUNK * j + CHUNK)
            weight = jnp.exp(scores[:, cols] - top)
            mass = mass + jnp.sum(weight, axis=1, keepdims=True)
            mixed = mixed + jnp.dot(weight.astype(BF16), kv[s, 1, cols, :], preferred_element_type=F32)
        og[:, 0:HD] = (mixed / mass).astype(BF16)
        if s == 0:
            pair_all(2)
        else:
            for half in range(2):
                for d in (1, 2, 3):
                    rs1(s - 1, half, d).wait_send()
                    rs2(s - 1, half, d).wait_send()
        for n in range(4):
            half, first = n // 2, 384 * (n % 2)
            cols = slice(384 * n, 384 * n + 384)
            upper = slice(HALF + 384 * n, HALF + 384 * n + 384)
            low = lax.dot_general(og[...], wo[cols, :], NT, preferred_element_type=F32)
            high = lax.dot_general(og[...], wo[upper, :], NT, preferred_element_type=F32)
            for q in range(CHIPS):
                rows = slice(8 * q, 8 * q + 8)
                spot = 16 * (q if half == 0 else 4 * (q % 4) + q // 4)
                both = jnp.concatenate([low[rows], high[rows]], axis=0).astype(BF16)
                tsend[half, spot : spot + 16, first : first + 384] = both
            if n % 2 == 1:
                for d in (1, 3, 2):
                    rs1(s, half, d).start()
        if s < STEPS - 1:
            kv_stage(s, 1)
        rs_middle(s)
        if s < STEPS - 1:
            kv_stage(s, 2)
        total = rs_end(s)
        level = [sigma(jnp.full((16, HD), times[s + i].astype(F32))) for i in range(2)]
        gap = (level[1] - level[0])[:, 0:1]
        xp[...] = xp[...] + gap * total
        if s < STEPS - 1:
            ag_start(s + 1)
            kv_stage(s, 3)
            ag_forward(s + 1)
            for half in range(2):
                ag_end(s + 1, half)
                unpack(s + 1, half)

    for r in range(CHIPS):
        k = r // 2
        first = 384 * (k % 4) + HD * (r % 2)
        fs[r] = xp[8 * (k // 4) : 8 * (k // 4) + 8, first : first + 256]

    def f_copy(r):
        rows = pl.ds(pl.multiple_of(me * 8, 8), 8)
        return remote(fs.at[r], fl.at[rows, :], f_s.at[r], f_r.at[me], (c * Z + z, r))

    def f_self():
        rows = pl.ds(pl.multiple_of(me * 8, 8), 8)
        return pltpu.make_async_copy(fs.at[head], fl.at[rows, :], f_r.at[me])

    def f_start(o, carry):
        r = lax.rem(head + o, CHIPS)
        f_copy(r).start()
        return carry

    lax.fori_loop(1, CHIPS, f_start, 0)

    @pl.when(natural)
    def _():
        f_self().start()

    @pl.when(jnp.logical_not(natural))
    def _():
        f_copy(head).start()

    def f_wait(q, carry):
        rows = pl.ds(pl.multiple_of(q * 8, 8), 8)
        remote(fs.at[0], fl.at[rows, :], f_s.at[0], f_r.at[q], partner).wait_recv()
        return carry

    lax.fori_loop(0, CHIPS, f_wait, 0)
    xt[...] = fl[...].T
    out[...] = xt[place, :]

    def all_sent(o, carry):
        remote(xs.at[0], xl.at[0], x_s.at[lax.rem(me + o, CHIPS)], x_r.at[0], partner).wait_send()
        f_copy(lax.rem(head + o, CHIPS)).wait_send()
        return carry

    lax.fori_loop(1, CHIPS, all_sent, 0)
    for s in range(STEPS):
        ag_sent(s)
    for s in range(STEPS - 1):
        kv_sent_rest(s)
    for half in range(2):
        for d in (1, 2, 3):
            rs1(STEPS - 1, half, d).wait_send()
            rs2(STEPS - 1, half, d).wait_send()

    @pl.when(jnp.logical_not(natural))
    def _():
        x_copy(me, partner).wait_send()
        f_copy(head).wait_send()
        for i, (src, here, there) in enumerate(shard_parts()):
            remote(src, there, swap_s.at[i], swap_r.at[i], twin).wait_send()

    def ring_sent(k, carry):
        for j in range(3):
            for d in range(2):
                ring_copy(j, d, k, z).wait_send()
        return carry

    lax.fori_loop(0, 7, ring_sent, 0)
    for j in range(3):
        for d in range(2):
            ring_copy(j, d, 7, z, d).wait_send()

    def pair_sent(zz, carry):
        for j in range(3):
            pair_copy(j, zz).wait_send()
        return carry

    lax.fori_loop(0, Z, pair_sent, 0)


def on_device(
    state, mod_weight, w_qkv, q_gain, k_gain, w_in, w_attn, w_out, cache_keys, cache_values, timesteps
):
    vmem = pl.BlockSpec(memory_space=pltpu.VMEM)
    hbm = pl.BlockSpec(memory_space=pl.ANY)
    smem = pl.BlockSpec(memory_space=pltpu.SMEM)
    dma = pltpu.SemaphoreType.DMA
    result = pl.pallas_call(
        kernel,
        out_shape=jax.ShapeDtypeStruct((192, TOK), F32),
        in_specs=[smem, vmem, vmem, hbm, hbm, hbm, hbm, hbm, hbm, hbm, hbm],
        out_specs=vmem,
        scratch_shapes=[
            pltpu.VMEM((D, 384), BF16),
            pltpu.VMEM((D, 384), BF16),
            pltpu.VMEM((D, 512), BF16),
            pltpu.VMEM((STEPS, 2, KEYS, HD), BF16),
            pltpu.VMEM((STEPS, 2, CHIPS * 16, PART), BF16),
            pltpu.VMEM((STEPS, 2, 3, 64, PART), BF16),
            pltpu.VMEM((STEPS, 2, 3, 16, PART), BF16),
            pltpu.VMEM((2, CHIPS * 16, PART), BF16),
            pltpu.VMEM((2, 64, PART), BF16),
            pltpu.VMEM((TOK, D), BF16),
            pltpu.VMEM((TOK, 512), BF16),
            pltpu.VMEM((TOK, KEYS), F32),
            pltpu.VMEM((CHIPS, 16, 256), F32),
            pltpu.VMEM((CHIPS, 16, 256), F32),
            pltpu.VMEM((CHIPS, 8, 256), F32),
            pltpu.VMEM((TOK, 256), F32),
            pltpu.VMEM((256, TOK), F32),
            pltpu.VMEM((2, 256, 256), BF16),
            pltpu.VMEM((6, 16, HALF), F32),
            pltpu.VMEM((16, HALF), F32),
            pltpu.VMEM((2, 1, HD), F32),
            dma((4,)), dma((4,)), dma((4,)), dma((4,)),
            dma((3, 2, 8)), dma((3, 2, 8)), dma((3, Z)), dma((3, Z)),
            dma((2, 2, 4, 2)), dma((2, 2, 4, 2)), dma((2, Z)), dma((2, Z)),
            dma((CHIPS,)), dma((CHIPS,)),
            dma((STEPS, 2, 4)), dma((STEPS, 2, 4)), dma((STEPS, 2, 16)), dma((STEPS, 2, 16)),
            dma((STEPS, 2, 4)), dma((STEPS, 2, 4)), dma((STEPS, 2, 4)), dma((STEPS, 2, 4)),
            dma((CHIPS,)), dma((CHIPS,)), dma((4,)),
        ],
        compiler_params=pltpu.CompilerParams(
            collective_id=0, has_side_effects=True, vmem_limit_bytes=60 * 1024 * 1024
        ),
    )(
        timesteps,
        state.T,
        jnp.transpose(mod_weight, (1, 2, 0)),
        w_qkv.reshape(ROWS, 384),
        w_in,
        w_attn.T,
        w_out.T,
        q_gain,
        k_gain,
        cache_keys.reshape(KEYS, HD),
        cache_values.reshape(KEYS, HD),
    )
    return result.T


def solution(mesh):
    in_specs = (
        P("patch", "head"),
        P(None, None, "head"),
        P("patch", "head", None),
        P("head", None),
        P("head", None),
        P("patch", "head"),
        P("head", "patch"),
        P("head", "patch"),
        P(None, "head", None),
        P(None, "head", None),
        P(),
    )
    return jax.shard_map(
        on_device, mesh=mesh, in_specs=in_specs, out_specs=P("patch", "head"), check_vma=False
    )
```

```python
import math

import jax
import jax.numpy as jnp
from jax import lax
from jax.experimental import pallas as pl
from jax.experimental.pallas import tpu as pltpu
from jax.sharding import PartitionSpec as P

MESH = pl.DeviceIdType.MESH
F32 = jnp.float32
BF16 = jnp.bfloat16
SCHED = 1000
STEPS = 3
Z = 16
CHIPS = 16
TOK = 128
D = 3072
HALF = D // 2
PART = HALF // 2
HD = 128
ROWS = 96
KEYS = 4096
CHUNK = 512
NT = (((1,), (1,)), ((), ()))


def sigma(unit_index):
    unit = 1.0 - unit_index / SCHED
    return 3.0 * unit / (1.0 + 2.0 * unit)


def kernel(
    times, state, mod_w, w_qkv, w_in, w_attn, w_out, q_gain, k_gain, cache_k, cache_v,
    out,
    wq, wi, wo, kv, hland, r1, r2, tsend, p2, hb, og, scores, xs, xl, fs, fl, tt, ft, xt, mw, modp, xp, gains,
    cache_s, cache_r, swap_s, swap_r, first_s, ring_s, ring_r, pair_s, pair_r,
    kring_s, kring_r, kpair_r, x_s, x_r, ag_s, ag1_r, ag2_r,
    rs1_s, rs1_r, rs2_s, rs2_r, f_s, f_r, t_s, t_r, local,
):
    patch = lax.axis_index("patch")
    head = lax.axis_index("head")
    yl, z = lax.div(patch, Z), lax.rem(patch, Z)
    yh, x, c = lax.div(head, 8), lax.rem(lax.div(head, 2), 4), lax.rem(head, 2)
    y = yh * 2 + yl
    me = y * 4 + x
    own = c * Z + z
    natural = c == yl

    def dev(yy, xx, cc, zz):
        return (lax.rem(yy, 2) * Z + zz, lax.div(yy, 2) * 8 + xx * 2 + cc)

    def chip_at(o):
        return lax.rem(y + lax.div(o, 4), 4), lax.rem(x + lax.rem(o, 4), 4)

    def remote(src, dst, send, recv, device):
        return pltpu.make_async_remote_copy(
            src_ref=src, dst_ref=dst, send_sem=send, recv_sem=recv, device_id=device, device_id_type=MESH
        )

    partner = dev(y, x, 1 - c, z)

    def wait_bytes(block, sem):
        pltpu.make_async_copy(block, block, sem).wait()

    z_next = (dev(y, x, c, lax.rem(z + 1, Z)), dev(y, x, c, lax.rem(z + Z - 1, Z)))
    z_far = (dev(y, x, c, lax.rem(z + 2, Z)), dev(y, x, c, lax.rem(z + Z - 2, Z)))
    twin = dev(yh * 2 + c, x, yl, z)
    twin_next = (dev(yh * 2 + c, x, yl, lax.rem(z + 1, Z)), dev(yh * 2 + c, x, yl, lax.rem(z + Z - 1, Z)))

    barrier = pltpu.get_barrier_semaphore()

    def greet(device):
        pl.semaphore_signal(barrier, inc=1, device_id=device, device_id_type=MESH)

    for device in z_next + z_far + twin_next:
        greet(device)
    rows_y = [lax.rem(y + d, 4) for d in range(4)]
    rows_x = [lax.rem(x + d, 4) for d in range(4)]
    greet(partner)
    for o in range(1, CHIPS):
        for core in range(2):
            greet(dev(rows_y[o // 4], rows_x[o % 4], core, z))

    weights = (wq, wi, wo)

    def slab(j, zz, half=None):
        start, size = (c * Z + zz) * ROWS, ROWS
        if half is not None:
            start, size = start + half * (ROWS // 2), ROWS // 2
        return weights[j].at[pl.ds(pl.multiple_of(start, 16), size), :]

    def shard(i, block):
        rows = pl.ds(pl.multiple_of(block * ROWS, 16), ROWS)
        return (
            (w_qkv, wq.at[rows, :]),
            (w_in, wi.at[rows, :]),
            (w_attn, wo.at[rows, 0:HD]),
            (w_out, wo.at[rows, HD:512]),
        )[i]

    def caches():
        return (
            (cache_k, kv.at[0, 0]),
            (cache_v, kv.at[0, 1]),
            (q_gain, gains.at[0]),
            (k_gain, gains.at[1]),
        )

    place = pl.ds(pl.multiple_of(c * 64, 64), 192)
    mw[...] = jnp.zeros_like(mw)
    xt[...] = jnp.zeros_like(xt)
    loads = [
        pltpu.make_async_copy(state, xt.at[place, :], local.at[0]),
        pltpu.make_async_copy(mod_w, mw.at[:, place, :], local.at[1]),
    ]
    for load in loads:
        load.start()

    pl.semaphore_wait(barrier, 37)

    for d in range(2):
        src, dst = shard(0, patch)
        remote(src, dst, first_s, ring_r.at[0, d, 0], twin_next[d]).start()
    part_of = (0, 1, 2, 2)

    @pl.when(natural)
    def _():
        for i in (1, 2, 3, 0):
            src, dst = shard(i, patch)
            pltpu.make_async_copy(src, dst, swap_r.at[part_of[i]]).start()
        for i, (src, dst) in enumerate(caches()):
            pltpu.make_async_copy(src, dst, cache_r.at[i // 2]).start()
            remote(src, dst, cache_s.at[i // 2], cache_r.at[i // 2], partner).start()

    @pl.when(jnp.logical_not(natural))
    def _():
        for i in (1, 2, 3, 0):
            src, dst = shard(i, patch)
            remote(src, dst, swap_s, swap_r.at[part_of[i]], twin).start()

    def pair_copy(j, zz):
        part = slab(j, zz)
        return remote(part, part, pair_s.at[j], pair_r.at[j], partner)

    def ring_copy(j, d, k, zz, half=None):
        block = slab(j, zz, half)
        return remote(block, block, ring_s.at[j], ring_r.at[j, d, lax.rem(k, 2)], z_next[d])

    def source(d, k):
        return lax.rem(z + Z - k, Z) if d == 0 else lax.rem(z + k, Z)

    def ring_start(j):
        wait_bytes(slab(j, z), swap_r.at[j])
        if j > 0:
            for d in range(2):
                ring_copy(j, d, 0, z).start()
        pair_copy(j, z).start()

    def ring_hop(k, last=False):
        for j in range(3):
            for d in range(2):
                ring_copy(j, d, k - 1, source(d, k)).wait_recv()
            for d in range(2):
                ring_copy(j, d, k, source(d, k), d if last else None).start()
            for d in range(2):
                pair_copy(j, source(d, k)).start()

    def ring_end(j):
        zz = source(0, 8)
        for d in range(2):
            ring_copy(j, d, 7, zz, d).wait_recv()
        pair_copy(j, zz).start()

    def pair_all(j):
        rows = pl.ds(pl.multiple_of((1 - c) * Z * ROWS, 16), Z * ROWS)
        wait_bytes(weights[j].at[rows, :], pair_r.at[j])

    for j in (1, 2, 0):
        ring_start(j)

    row = lax.broadcasted_iota(jnp.int32, (8, HD), 0)
    lane = lax.broadcasted_iota(jnp.int32, (8, HD), 1)
    stepped = lax.rem(row, 3)
    when = jnp.zeros((8, HD), F32)
    for s in range(STEPS):
        when = jnp.where(stepped == s, times[s].astype(F32), when)
    freq = jnp.exp(-math.log(10000.0) * lane.astype(F32) / HD)
    angle = 1000.0 * sigma(when) * freq
    emb = jnp.concatenate([jnp.cos(angle), jnp.sin(angle)], axis=1).astype(BF16)
    for load in loads:
        load.wait()
    mods = [lax.dot_general(emb, mw[j], NT, preferred_element_type=F32) for j in range(2)]
    row2 = lax.broadcasted_iota(jnp.int32, (8, 256), 0)
    mod_rows = jnp.where(row2 < 3, mods[0], mods[1])
    rows_here = xt[...].T
    for q in range(CHIPS):
        xs[q, 0:8] = rows_here[8 * q : 8 * q + 8]
        xs[q, 8:16] = mod_rows

    def x_copy(q, device):
        return remote(xs.at[q], xl.at[head], x_s, x_r, device)

    @pl.when(natural)
    def _():
        pltpu.make_async_copy(xs.at[me], xl.at[head], x_r).start()

    @pl.when(jnp.logical_not(natural))
    def _():
        x_copy(me, partner).start()

    def x_start(o, carry):
        yy, xx = chip_at(o)
        x_copy(yy * 4 + xx, dev(yy, xx, yl, z)).start()
        return carry

    lax.fori_loop(1, CHIPS, x_start, 0)

    def loop_hops(lo, hi):
        def body(k, carry):
            ring_hop(k)
            return carry

        lax.fori_loop(lo, hi, body, 0)

    loop_hops(1, 4)
    wait_bytes(xl, x_r)
    for k in range(8):
        a, b = xl[2 * k], xl[2 * k + 1]
        group = jnp.concatenate([a[:, :HD], a[:, HD:] + b[:, :HD], b[:, HD:]], axis=1)
        rows, cols = slice(8 * (k // 4), 8 * (k // 4) + 8), slice(384 * (k % 4), 384 * (k % 4) + 384)
        xp[rows, cols] = group[0:8]
        for i in range(6):
            modp[i, rows, cols] = jnp.broadcast_to(group[8 + i : 9 + i], (8, 384))

    def fold(sums):
        total = (sums[0:8] + sums[8:16]) * (1.0 / D)
        return jnp.concatenate([total, total], axis=0)

    def turn(i, d):
        return lax.rem(i + d, 4)

    def slot(yy, xx):
        return pl.ds(pl.multiple_of((yy * 4 + xx) * 16, 16), 16)

    def line(half, d):
        return dev(y, turn(x, d), c, z) if half == 0 else dev(turn(y, d), x, c, z)

    def origin(half, d):
        return slot(y, turn(x, 4 - d)) if half == 0 else slot(turn(y, 4 - d), x)

    def ag1(s, half, d, rows):
        block = hland.at[s, half, rows, :]
        return remote(block, block, ag_s, ag1_r.at[half, d - 1], line(half, d))

    def ag2(s, half, d, rows):
        block = hland.at[s, half, rows, :]
        return remote(block, block, ag_s, ag2_r.at[half], line(1 - half, d))

    def ag_start(s):
        rows = xp[...]
        delta = rows - fold(jnp.sum(rows, axis=1, keepdims=True))
        var = fold(jnp.sum(delta * delta, axis=1, keepdims=True))
        h = (delta * lax.rsqrt(var + 1e-06) * (1.0 + modp[s]) + modp[3 + s]).astype(BF16)
        mine = slot(y, x)
        for half in range(2):
            hland[s, half, mine, :] = h[:, half * PART : half * PART + PART]
        for d in (1, 3, 2):
            for half in range(2):
                ag1(s, half, d, mine).start()
        for d in (1, 3, 2):
            for half in range(2):
                ag2(s, half, d, mine).start()

    def ag_forward(s):
        for d in (1, 3, 2):
            for half in range(2):
                rows = origin(half, d)
                ag1(s, half, d, rows).wait_recv()
                for e in (1, 3, 2):
                    ag2(s, half, e, rows).start()

    def ag_end(s, half):
        wait_bytes(hland.at[s, half, 0:192, :], ag2_r.at[half])

    def ag_sent(s):
        wait_bytes(hland.at[s, :, 0:240, :], ag_s)

    def rs1(s, half, d):
        to = turn(y if half == 0 else x, d)
        block = tsend.at[half, pl.ds(pl.multiple_of(to * 64, 64), 64), :]
        return remote(
            block, r1.at[s, half, d - 1], rs1_s.at[half], rs1_r.at[half], line(1 - half, d)
        )

    def rs2(s, half, d):
        to = turn(x if half == 0 else y, d)
        block = p2.at[half, pl.ds(pl.multiple_of(to * 16, 16), 16), :]
        return remote(
            block, r2.at[s, half, d - 1], rs2_s.at[half], rs2_r.at[half], line(half, d)
        )

    def rs_middle(s):
        for half in range(2):
            here = pl.ds(pl.multiple_of((y if half == 0 else x) * 64, 64), 64)
            wait_bytes(r1.at[s, half], rs1_r.at[half])
            part = tsend[half, here, :].astype(F32)
            for d in range(3):
                part = part + r1[s, half, d].astype(F32)
            p2[half] = part.astype(BF16)
            for d in (1, 3, 2):
                rs2(s, half, d).start()

    def rs_sent():
        for half in range(2):
            wait_bytes(r1.at[0, half], rs1_s.at[half])
            wait_bytes(r2.at[0, half], rs2_s.at[half])

    def rs_end(s):
        parts = []
        for half in range(2):
            here = pl.ds(pl.multiple_of((x if half == 0 else y) * 16, 16), 16)
            wait_bytes(r2.at[s, half], rs2_r.at[half])
            part = p2[half, here, :].astype(F32)
            for d in (1, 3, 2):
                part = part + r2[s, half, d - 1].astype(F32)
            parts.append(part)
        return jnp.concatenate(parts, axis=1)

    def unpack(s, half):
        for m in range(8):
            block = hland[s, half, 32 * m : 32 * m + 32, :].astype(F32)
            rows = slice(16 * m, 16 * m + 16)
            low, high = half * PART, HALF + half * PART
            hb[rows, low : low + PART] = jnp.concatenate([block[0:8], block[16:24]], axis=0).astype(BF16)
            hb[rows, high : high + PART] = jnp.concatenate([block[8:16], block[24:32]], axis=0).astype(BF16)

    ag_start(0)
    loop_hops(4, 5)
    ag_forward(0)
    loop_hops(5, 7)
    for half in range(2):
        ag_end(0, half)
        unpack(0, half)
    ring_hop(7, last=True)
    ring_end(0)
    ring_end(1)
    pair_all(0)

    wait_bytes(kv.at[0], cache_r.at[0])
    wait_bytes(gains, cache_r.at[1])

    def kv_block(s, cc, zz, part=None):
        start, size = (cc * Z + zz) * TOK, TOK
        if part is not None:
            start, size = start + part * (TOK // 2), TOK // 2
        return kv.at[s + 1, :, pl.ds(pl.multiple_of(start, 16), size), :]

    def kring_copy(s, d, k, far, zz, part=None):
        block = kv_block(s, c, zz, part)
        device = z_far[d] if far else z_next[d]
        return remote(block, block, kring_s.at[s, min(k, 1)], kring_r.at[s, d, k, far], device)

    def kpair_copy(s, zz, rest=1):
        block = kv_block(s, c, zz)
        return remote(block, block, kring_s.at[s, rest], kpair_r.at[s], partner)

    def kv_send(s, k):
        for d in range(2):
            kring_copy(s, d, k, 1, source(d, 2 * k), d if k == 3 else None).start()
        for d in range(2):
            kring_copy(s, d, k, 0, source(d, 2 * k)).start()

    def kv_start(s):
        kv_send(s, 0)
        kpair_copy(s, z, 0).start()

    def kv_stage(s, k):
        for d in range(2):
            kring_copy(s, d, k - 1, 1, source(d, 2 * k), d if k == 4 else None).wait_recv()
        if k < 4:
            kv_send(s, k)
            for d in range(2):
                kpair_copy(s, source(d, 2 * k)).start()
        else:
            kpair_copy(s, source(0, 8)).start()
        for d in range(2):
            zz = source(d, 2 * k - 1)
            kring_copy(s, d, k - 1, 0, zz).wait_recv()
            kpair_copy(s, zz).start()

    def kv_wait(s):
        rows = pl.ds(pl.multiple_of((1 - c) * Z * TOK, 16), Z * TOK)
        wait_bytes(kv.at[s + 1, :, rows, :], kpair_r.at[s])

    def kv_sent_own(s):
        wait_bytes(kv.at[s + 1, :, 0 : 5 * TOK, :], kring_s.at[s, 0])

    def kv_sent_rest(s):
        wait_bytes(kv.at[s + 1, :, 0 : 26 * TOK, :], kring_s.at[s, 1])

    def rms(values, gain):
        return values * lax.rsqrt(jnp.mean(values * values, axis=1, keepdims=True) + 1e-06) * gain

    def f_copy(r):
        rows = pl.ds(pl.multiple_of(me * 8, 8), 8)
        return remote(fs.at[r], fl.at[rows, :], f_s, f_r, (c * Z + z, r))

    def f_self():
        rows = pl.ds(pl.multiple_of(me * 8, 8), 8)
        return pltpu.make_async_copy(fs.at[head], fl.at[rows, :], f_r)

    def f_start():
        for r in range(CHIPS):
            k = r // 2
            first = 384 * (k % 4) + HD * (r % 2)
            fs[r] = xp[8 * (k // 4) : 8 * (k // 4) + 8, first : first + 256]

        def body(o, carry):
            f_copy(lax.rem(head + o, CHIPS)).start()
            return carry

        lax.fori_loop(1, CHIPS, body, 0)

        @pl.when(natural)
        def _():
            f_self().start()

        @pl.when(jnp.logical_not(natural))
        def _():
            f_copy(head).start()

    def f_wait():
        wait_bytes(fl, f_r)
        xt[...] = fl[...].T

    def t_copy(r):
        return remote(tt.at[r], ft.at[me], t_s, t_r, (c * Z + z, r))

    own_rows = pl.ds(pl.multiple_of(own * TOK, 16), TOK)

    for s in range(STEPS):
        qkv = jnp.dot(hb[...], wq[...], preferred_element_type=F32)
        query = rms(qkv[:, 0:HD], gains[0]).astype(BF16)
        fresh = (rms(qkv[:, HD : 2 * HD], gains[1]).astype(BF16), qkv[:, 2 * HD :].astype(BF16))
        if s > 0:
            kv_sent_own(s - 1)
        for i in range(2):
            old = kv[s, i, own_rows, :].astype(F32)
            if s < STEPS - 1:
                change = (fresh[i].astype(F32) - old).astype(BF16)
                kv[s + 1, i, own_rows, :] = (old + change.astype(F32)).astype(BF16)
            kv[s, i, own_rows, :] = fresh[i]
        if s < STEPS - 1:
            kv_start(s)
        if s == 0:
            pair_all(1)
        og[:, HD:512] = jax.nn.gelu(
            jnp.dot(hb[...], wi[...], preferred_element_type=F32), approximate=True
        ).astype(BF16)
        if s == 0:
            ring_end(2)
        else:
            kv_stage(s - 1, 4)
            kv_wait(s - 1)
        top = jnp.full((TOK, 1), -jnp.inf, F32)
        for j in range(KEYS // CHUNK):
            cols = slice(CHUNK * j, CHUNK * j + CHUNK)
            score = lax.dot_general(query, kv[s, 0, cols, :], NT, preferred_element_type=F32)
            score = score * (1.0 / math.sqrt(HD))
            scores[:, cols] = score
            top = jnp.maximum(top, jnp.max(score, axis=1, keepdims=True))
        mass = jnp.zeros((TOK, 1), F32)
        mixed = jnp.zeros((TOK, HD), F32)
        for j in range(KEYS // CHUNK):
            cols = slice(CHUNK * j, CHUNK * j + CHUNK)
            weight = jnp.exp(scores[:, cols] - top)
            mass = mass + jnp.sum(weight, axis=1, keepdims=True)
            mixed = mixed + jnp.dot(weight.astype(BF16), kv[s, 1, cols, :], preferred_element_type=F32)
        og[:, 0:HD] = (mixed / mass).astype(BF16)
        if s == 0:
            pair_all(2)
        elif s < STEPS - 1:
            rs_sent()
        level = [sigma(jnp.full((16, HD), times[s + i].astype(F32))) for i in range(2)]
        gap = (level[1] - level[0])[:, 0:1]
        if s == STEPS - 1:
            break
        for n in range(4):
            half, first = n // 2, 384 * (n % 2)
            cols = slice(384 * n, 384 * n + 384)
            upper = slice(HALF + 384 * n, HALF + 384 * n + 384)
            low = lax.dot_general(og[...], wo[cols, :], NT, preferred_element_type=F32)
            high = lax.dot_general(og[...], wo[upper, :], NT, preferred_element_type=F32)
            for q in range(CHIPS):
                rows = slice(8 * q, 8 * q + 8)
                spot = 16 * (q if half == 0 else 4 * (q % 4) + q // 4)
                both = jnp.concatenate([low[rows], high[rows]], axis=0).astype(BF16)
                tsend[half, spot : spot + 16, first : first + 384] = both
            if n % 2 == 1:
                for d in (1, 3, 2):
                    rs1(s, half, d).start()
        kv_stage(s, 1)
        rs_middle(s)
        kv_stage(s, 2)
        xp[...] = xp[...] + gap * rs_end(s)
        ag_sent(s)
        ag_start(s + 1)
        kv_stage(s, 3)
        ag_forward(s + 1)
        if s == STEPS - 2:
            f_start()
        for half in range(2):
            ag_end(s + 1, half)
            unpack(s + 1, half)

    for g in range(4):
        group = lax.rem(lax.div(head, 4) + g, 4)
        features = pl.ds(pl.multiple_of(group * 768, 16), 768)
        term = lax.dot_general(wo[features, :], og[...], NT, preferred_element_type=F32).astype(BF16)
        for i in range(4):
            r = group * 4 + i
            tt[r] = term[192 * i : 192 * i + 192]

            @pl.when(jnp.logical_and(natural, r == head))
            def _():
                pltpu.make_async_copy(tt.at[r], ft.at[me], t_r).start()

            @pl.when(jnp.logical_not(jnp.logical_and(natural, r == head)))
            def _():
                t_copy(r).start()

    f_wait()
    wait_bytes(ft, t_r)
    total = jnp.zeros((192, TOK), F32)
    for q in range(CHIPS):
        total = total + ft[q].astype(F32)
    out[...] = xt[place, :] + gap[0:1, 0:1] * total

    rs_sent()
    ag_sent(STEPS - 1)
    for s in range(STEPS - 1):
        kv_sent_rest(s)
    for j in range(3):
        wait_bytes(weights[j].at[0 : Z * ROWS, :], pair_s.at[j])
        wait_bytes(weights[j].at[0 : (15 if j > 0 else 13) * ROWS, :], ring_s.at[j])
    wait_bytes(wq.at[0 : 2 * ROWS, :], first_s)

    @pl.when(natural)
    def _():
        wait_bytes(xs.at[0:15], x_s)
        wait_bytes(fs.at[0:15], f_s)
        wait_bytes(tt.at[0:15], t_s)
        wait_bytes(kv.at[0], cache_s.at[0])
        wait_bytes(gains, cache_s.at[1])

    @pl.when(jnp.logical_not(natural))
    def _():
        wait_bytes(xs, x_s)
        wait_bytes(fs, f_s)
        wait_bytes(tt, t_s)
        wait_bytes(wo.at[0:240, :], swap_s)


def on_device(
    state, mod_weight, w_qkv, q_gain, k_gain, w_in, w_attn, w_out, cache_keys, cache_values, timesteps
):
    vmem = pl.BlockSpec(memory_space=pltpu.VMEM)
    hbm = pl.BlockSpec(memory_space=pl.ANY)
    smem = pl.BlockSpec(memory_space=pltpu.SMEM)
    dma = pltpu.SemaphoreType.DMA
    one = pltpu.SemaphoreType.DMA
    result = pl.pallas_call(
        kernel,
        out_shape=jax.ShapeDtypeStruct((192, TOK), F32),
        in_specs=[smem, hbm, hbm, hbm, hbm, hbm, hbm, hbm, hbm, hbm, hbm],
        out_specs=vmem,
        scratch_shapes=[
            pltpu.VMEM((D, 384), BF16),
            pltpu.VMEM((D, 384), BF16),
            pltpu.VMEM((D, 512), BF16),
            pltpu.VMEM((STEPS, 2, KEYS, HD), BF16),
            pltpu.VMEM((STEPS, 2, CHIPS * 16, PART), BF16),
            pltpu.VMEM((STEPS, 2, 3, 64, PART), BF16),
            pltpu.VMEM((STEPS, 2, 3, 16, PART), BF16),
            pltpu.VMEM((2, CHIPS * 16, PART), BF16),
            pltpu.VMEM((2, 64, PART), BF16),
            pltpu.VMEM((TOK, D), BF16),
            pltpu.VMEM((TOK, 512), BF16),
            pltpu.VMEM((TOK, KEYS), F32),
            pltpu.VMEM((CHIPS, 16, 256), F32),
            pltpu.VMEM((CHIPS, 16, 256), F32),
            pltpu.VMEM((CHIPS, 8, 256), F32),
            pltpu.VMEM((TOK, 256), F32),
            pltpu.VMEM((CHIPS, 192, TOK), BF16),
            pltpu.VMEM((CHIPS, 192, TOK), BF16),
            pltpu.VMEM((256, TOK), F32),
            pltpu.VMEM((2, 256, 256), BF16),
            pltpu.VMEM((6, 16, HALF), F32),
            pltpu.VMEM((16, HALF), F32),
            pltpu.VMEM((2, 1, HD), F32),
            dma((2,)), dma((2,)), one, dma((3,)), one, dma((3,)), dma((3, 2, 2)), dma((3,)), dma((3,)),
            dma((2, 2)), dma((2, 2, 4, 2)), dma((2,)), one, one, one, dma((2, 3)), dma((2,)),
            dma((2,)), dma((2,)), dma((2,)), dma((2,)), one, one, one, one, dma((2,)),
        ],
        compiler_params=pltpu.CompilerParams(
            collective_id=0, has_side_effects=True, vmem_limit_bytes=60 * 1024 * 1024
        ),
    )(
        timesteps,
        state.T,
        jnp.transpose(mod_weight, (1, 2, 0)),
        w_qkv.reshape(ROWS, 384),
        w_in,
        w_attn.T,
        w_out.T,
        q_gain,
        k_gain,
        cache_keys.reshape(KEYS, HD),
        cache_values.reshape(KEYS, HD),
    )
    return result.T


def solution(mesh):
    in_specs = (
        P("patch", "head"),
        P(None, None, "head"),
        P("patch", "head", None),
        P("head", None),
        P("head", None),
        P("patch", "head"),
        P("head", "patch"),
        P("head", "patch"),
        P(None, "head", None),
        P(None, "head", None),
        P(),
    )
    return jax.shard_map(
        on_device, mesh=mesh, in_specs=in_specs, out_specs=P("patch", "head"), check_vma=False
    )
```

```python
import math

import jax
import jax.numpy as jnp
from jax import lax
from jax.experimental import pallas as pl
from jax.experimental.pallas import tpu as pltpu
from jax.sharding import PartitionSpec as P

MESH = pl.DeviceIdType.MESH
F32 = jnp.float32
BF16 = jnp.bfloat16
SCHED = 1000
STEPS = 3
Z = 16
CHIPS = 16
TOK = 128
D = 3072
HALF = D // 2
PART = HALF // 2
HD = 128
ROWS = 96
KEYS = 4096
CHUNK = 512
NT = (((1,), (1,)), ((), ()))


def sigma(unit_index):
    unit = 1.0 - unit_index / SCHED
    return 3.0 * unit / (1.0 + 2.0 * unit)


def kernel(
    times, state, mod_w, w_qkv, w_in, w_attn, w_out, q_gain, k_gain, cache_k, cache_v,
    out,
    wq, wi, wo, kv, hland, r1, r2, tsend, p2, hb, og, scores, xs, xl, fs, fl, tt, ft, xt, mw, modp, xp, gains,
    cache_s, cache_r, swap_s, swap_r, first_s, ring_s, ring_r, pair_s, pair_r,
    kring_s, kring_r, kpair_r, x_s, x_r, ag_s, ag1_r, ag2_r,
    rs1_s, rs1_r, rs2_s, rs2_r, f_s, f_r, t_s, t_r, local,
):
    patch = lax.axis_index("patch")
    head = lax.axis_index("head")
    yl, z = lax.div(patch, Z), lax.rem(patch, Z)
    yh, x, c = lax.div(head, 8), lax.rem(lax.div(head, 2), 4), lax.rem(head, 2)
    y = yh * 2 + yl
    me = y * 4 + x
    own = c * Z + z
    natural = c == yl

    def dev(yy, xx, cc, zz):
        return (lax.rem(yy, 2) * Z + zz, lax.div(yy, 2) * 8 + xx * 2 + cc)

    def chip_at(o):
        return lax.rem(y + lax.div(o, 4), 4), lax.rem(x + lax.rem(o, 4), 4)

    def remote(src, dst, send, recv, device):
        return pltpu.make_async_remote_copy(
            src_ref=src, dst_ref=dst, send_sem=send, recv_sem=recv, device_id=device, device_id_type=MESH
        )

    partner = dev(y, x, 1 - c, z)

    def wait_bytes(block, sem):
        pltpu.make_async_copy(block, block, sem).wait()

    z_next = (dev(y, x, c, lax.rem(z + 1, Z)), dev(y, x, c, lax.rem(z + Z - 1, Z)))
    z_far = (dev(y, x, c, lax.rem(z + 2, Z)), dev(y, x, c, lax.rem(z + Z - 2, Z)))
    twin = dev(yh * 2 + c, x, yl, z)
    twin_next = (dev(yh * 2 + c, x, yl, lax.rem(z + 1, Z)), dev(yh * 2 + c, x, yl, lax.rem(z + Z - 1, Z)))

    barrier = pltpu.get_barrier_semaphore()

    def greet(device):
        pl.semaphore_signal(barrier, inc=1, device_id=device, device_id_type=MESH)

    for device in z_next + z_far + twin_next:
        greet(device)
    rows_y = [lax.rem(y + d, 4) for d in range(4)]
    rows_x = [lax.rem(x + d, 4) for d in range(4)]
    greet(partner)
    for o in range(1, CHIPS):
        for core in range(2):
            greet(dev(rows_y[o // 4], rows_x[o % 4], core, z))

    weights = (wq, wi, wo)

    def slab(j, zz, half=None):
        start, size = (c * Z + zz) * ROWS, ROWS
        if half is not None:
            start, size = start + half * (ROWS // 2), ROWS // 2
        return weights[j].at[pl.ds(pl.multiple_of(start, 16), size), :]

    def shard(i, block):
        rows = pl.ds(pl.multiple_of(block * ROWS, 16), ROWS)
        return (
            (w_qkv, wq.at[rows, :]),
            (w_in, wi.at[rows, :]),
            (w_attn, wo.at[rows, 0:HD]),
            (w_out, wo.at[rows, HD:512]),
        )[i]

    def caches():
        return (
            (cache_k, kv.at[0, 0]),
            (cache_v, kv.at[0, 1]),
            (q_gain, gains.at[0]),
            (k_gain, gains.at[1]),
        )

    place = pl.ds(pl.multiple_of(c * 64, 64), 192)
    mw[...] = jnp.zeros_like(mw)
    xt[...] = jnp.zeros_like(xt)
    loads = [
        pltpu.make_async_copy(state, xt.at[place, :], local.at[0]),
        pltpu.make_async_copy(mod_w, mw.at[:, place, :], local.at[1]),
    ]
    for load in loads:
        load.start()

    pl.semaphore_wait(barrier, 37)

    for half in range(2):
        for d in range(2):
            src = w_qkv.at[half * (ROWS // 2) : (half + 1) * (ROWS // 2), :]
            rows = pl.ds(pl.multiple_of(patch * ROWS + half * (ROWS // 2), 16), ROWS // 2)
            remote(src, wq.at[rows, :], first_s, ring_r.at[0, half, d, 0], twin_next[d]).start()
    part_of = (0, 1, 2, 2)

    @pl.when(natural)
    def _():
        for i in (1, 2, 3, 0):
            src, dst = shard(i, patch)
            pltpu.make_async_copy(src, dst, swap_r.at[part_of[i]]).start()
        for i, (src, dst) in enumerate(caches()):
            pltpu.make_async_copy(src, dst, cache_r.at[i // 2]).start()
            remote(src, dst, cache_s.at[i // 2], cache_r.at[i // 2], partner).start()

    @pl.when(jnp.logical_not(natural))
    def _():
        for i in (1, 2, 3, 0):
            src, dst = shard(i, patch)
            remote(src, dst, swap_s, swap_r.at[part_of[i]], twin).start()

    def pair_copy(j, zz):
        part = slab(j, zz)
        return remote(part, part, pair_s.at[j], pair_r.at[j], partner)

    def ring_copy(j, half, d, k, zz):
        block = slab(j, zz, half)
        return remote(block, block, ring_s.at[j], ring_r.at[j, half, d, lax.rem(k, 2)], z_next[d])

    def source(d, k):
        return lax.rem(z + Z - k, Z) if d == 0 else lax.rem(z + k, Z)

    def ring_start(j):
        wait_bytes(slab(j, z), swap_r.at[j])
        if j > 0:
            for half in range(2):
                for d in range(2):
                    ring_copy(j, half, d, 0, z).start()
        pair_copy(j, z).start()

    def ring_hop(j, k, last=False):
        for half in range(2):
            for d in range(2):
                ring_copy(j, half, d, k - 1, source(d, k)).wait_recv()
            for d in range(2):
                if not last or half == d:
                    ring_copy(j, half, d, k, source(d, k)).start()
        for d in range(2):
            pair_copy(j, source(d, k)).start()

    def ring_end(j):
        zz = source(0, 8)
        for d in range(2):
            ring_copy(j, d, d, 7, zz).wait_recv()
        pair_copy(j, zz).start()

    def pair_all(j):
        rows = pl.ds(pl.multiple_of((1 - c) * Z * ROWS, 16), Z * ROWS)
        wait_bytes(weights[j].at[rows, :], pair_r.at[j])

    for j in (1, 2, 0):
        ring_start(j)

    row = lax.broadcasted_iota(jnp.int32, (8, HD), 0)
    lane = lax.broadcasted_iota(jnp.int32, (8, HD), 1)
    stepped = lax.rem(row, 3)
    when = jnp.zeros((8, HD), F32)
    for s in range(STEPS):
        when = jnp.where(stepped == s, times[s].astype(F32), when)
    freq = jnp.exp(-math.log(10000.0) * lane.astype(F32) / HD)
    angle = 1000.0 * sigma(when) * freq
    emb = jnp.concatenate([jnp.cos(angle), jnp.sin(angle)], axis=1).astype(BF16)
    for load in loads:
        load.wait()
    mods = [lax.dot_general(emb, mw[j], NT, preferred_element_type=F32) for j in range(2)]
    row2 = lax.broadcasted_iota(jnp.int32, (8, 256), 0)
    mod_rows = jnp.where(row2 < 3, mods[0], mods[1])
    rows_here = xt[...].T
    for q in range(CHIPS):
        xs[q, 0:8] = rows_here[8 * q : 8 * q + 8]
        xs[q, 8:16] = mod_rows

    def x_copy(q, device):
        return remote(xs.at[q], xl.at[head], x_s, x_r, device)

    @pl.when(natural)
    def _():
        pltpu.make_async_copy(xs.at[me], xl.at[head], x_r).start()

    @pl.when(jnp.logical_not(natural))
    def _():
        x_copy(me, partner).start()

    def x_start(o, carry):
        yy, xx = chip_at(o)
        x_copy(yy * 4 + xx, dev(yy, xx, yl, z)).start()
        return carry

    lax.fori_loop(1, CHIPS, x_start, 0)

    def hop(k, carry):
        ring_hop(0, k)
        ring_hop(1, k)
        ring_hop(2, k)
        return carry

    ring_hop(0, 1)
    ring_hop(1, 1)
    ring_hop(2, 1)
    lax.fori_loop(2, 4, hop, 0)
    wait_bytes(xl, x_r)
    for k in range(8):
        a, b = xl[2 * k], xl[2 * k + 1]
        group = jnp.concatenate([a[:, :HD], a[:, HD:] + b[:, :HD], b[:, HD:]], axis=1)
        rows, cols = slice(8 * (k // 4), 8 * (k // 4) + 8), slice(384 * (k % 4), 384 * (k % 4) + 384)
        xp[rows, cols] = group[0:8]
        for i in range(6):
            modp[i, rows, cols] = jnp.broadcast_to(group[8 + i : 9 + i], (8, 384))

    def fold(sums):
        total = (sums[0:8] + sums[8:16]) * (1.0 / D)
        return jnp.concatenate([total, total], axis=0)

    def turn(i, d):
        return lax.rem(i + d, 4)

    def slot(yy, xx):
        return pl.ds(pl.multiple_of((yy * 4 + xx) * 16, 16), 16)

    def line(half, d):
        return dev(y, turn(x, d), c, z) if half == 0 else dev(turn(y, d), x, c, z)

    def origin(half, d):
        return slot(y, turn(x, 4 - d)) if half == 0 else slot(turn(y, 4 - d), x)

    def ag1(s, half, d, rows):
        block = hland.at[s, half, rows, :]
        return remote(block, block, ag_s, ag1_r.at[half, d - 1], line(half, d))

    def ag2(s, half, d, rows):
        block = hland.at[s, half, rows, :]
        return remote(block, block, ag_s, ag2_r.at[half], line(1 - half, d))

    def ag_start(s):
        rows = xp[...]
        delta = rows - fold(jnp.sum(rows, axis=1, keepdims=True))
        var = fold(jnp.sum(delta * delta, axis=1, keepdims=True))
        h = (delta * lax.rsqrt(var + 1e-06) * (1.0 + modp[s]) + modp[3 + s]).astype(BF16)
        mine = slot(y, x)
        for half in range(2):
            hland[s, half, mine, :] = h[:, half * PART : half * PART + PART]
        for d in (1, 3, 2):
            for half in range(2):
                ag1(s, half, d, mine).start()
        for d in (1, 3, 2):
            for half in range(2):
                ag2(s, half, d, mine).start()

    def ag_forward(s):
        for d in (1, 3, 2):
            for half in range(2):
                rows = origin(half, d)
                ag1(s, half, d, rows).wait_recv()
                for e in (1, 3, 2):
                    ag2(s, half, e, rows).start()

    def ag_end(s, half):
        wait_bytes(hland.at[s, half, 0:192, :], ag2_r.at[half])

    def ag_sent(s):
        wait_bytes(hland.at[s, :, 0:240, :], ag_s)

    def rs1(s, half, d):
        to = turn(y if half == 0 else x, d)
        block = tsend.at[half, pl.ds(pl.multiple_of(to * 64, 64), 64), :]
        return remote(
            block, r1.at[s, half, d - 1], rs1_s.at[half], rs1_r.at[half], line(1 - half, d)
        )

    def rs2(s, half, d):
        to = turn(x if half == 0 else y, d)
        block = p2.at[half, pl.ds(pl.multiple_of(to * 16, 16), 16), :]
        return remote(
            block, r2.at[s, half, d - 1], rs2_s.at[half], rs2_r.at[half], line(half, d)
        )

    def rs_middle(s):
        for half in range(2):
            here = pl.ds(pl.multiple_of((y if half == 0 else x) * 64, 64), 64)
            wait_bytes(r1.at[s, half], rs1_r.at[half])
            part = tsend[half, here, :].astype(F32)
            for d in range(3):
                part = part + r1[s, half, d].astype(F32)
            p2[half] = part.astype(BF16)
            for d in (1, 3, 2):
                rs2(s, half, d).start()

    def rs_sent():
        for half in range(2):
            wait_bytes(r1.at[0, half], rs1_s.at[half])
            wait_bytes(r2.at[0, half], rs2_s.at[half])

    def rs_end(s):
        parts = []
        for half in range(2):
            here = pl.ds(pl.multiple_of((x if half == 0 else y) * 16, 16), 16)
            wait_bytes(r2.at[s, half], rs2_r.at[half])
            part = p2[half, here, :].astype(F32)
            for d in (1, 3, 2):
                part = part + r2[s, half, d - 1].astype(F32)
            parts.append(part)
        return jnp.concatenate(parts, axis=1)

    def unpack(s, half):
        for m in range(8):
            block = hland[s, half, 32 * m : 32 * m + 32, :].astype(F32)
            rows = slice(16 * m, 16 * m + 16)
            low, high = half * PART, HALF + half * PART
            hb[rows, low : low + PART] = jnp.concatenate([block[0:8], block[16:24]], axis=0).astype(BF16)
            hb[rows, high : high + PART] = jnp.concatenate([block[8:16], block[24:32]], axis=0).astype(BF16)

    ag_start(0)
    lax.fori_loop(4, 5, hop, 0)
    ag_forward(0)
    lax.fori_loop(5, 7, hop, 0)
    for half in range(2):
        ag_end(0, half)
        unpack(0, half)
    ring_hop(0, 7, last=True)
    ring_hop(1, 7, last=True)
    ring_hop(2, 7, last=True)
    ring_end(0)
    ring_end(1)
    pair_all(0)

    wait_bytes(kv.at[0], cache_r.at[0])
    wait_bytes(gains, cache_r.at[1])

    def kv_block(s, cc, zz, part=None):
        start, size = (cc * Z + zz) * TOK, TOK
        if part is not None:
            start, size = start + part * (TOK // 2), TOK // 2
        return kv.at[s + 1, :, pl.ds(pl.multiple_of(start, 16), size), :]

    def kring_copy(s, d, k, far, zz, part=None):
        block = kv_block(s, c, zz, part)
        device = z_far[d] if far else z_next[d]
        return remote(block, block, kring_s.at[s, min(k, 1)], kring_r.at[s, d, k, far], device)

    def kpair_copy(s, zz, rest=1):
        block = kv_block(s, c, zz)
        return remote(block, block, kring_s.at[s, rest], kpair_r.at[s], partner)

    def kv_send(s, k):
        for d in range(2):
            kring_copy(s, d, k, 1, source(d, 2 * k), d if k == 3 else None).start()
        for d in range(2):
            kring_copy(s, d, k, 0, source(d, 2 * k)).start()

    def kv_start(s):
        kv_send(s, 0)
        kpair_copy(s, z, 0).start()

    def kv_stage(s, k):
        for d in range(2):
            kring_copy(s, d, k - 1, 1, source(d, 2 * k), d if k == 4 else None).wait_recv()
        if k < 4:
            kv_send(s, k)
            for d in range(2):
                kpair_copy(s, source(d, 2 * k)).start()
        else:
            kpair_copy(s, source(0, 8)).start()
        for near in (k - 1,):
            for d in range(2):
                zz = source(d, 2 * near + 1)
                kring_copy(s, d, near, 0, zz).wait_recv()
                kpair_copy(s, zz).start()

    def kv_wait(s):
        rows = pl.ds(pl.multiple_of((1 - c) * Z * TOK, 16), Z * TOK)
        wait_bytes(kv.at[s + 1, :, rows, :], kpair_r.at[s])

    def kv_sent_own(s):
        wait_bytes(kv.at[s + 1, :, 0 : 5 * TOK, :], kring_s.at[s, 0])

    def kv_sent_rest(s):
        wait_bytes(kv.at[s + 1, :, 0 : 26 * TOK, :], kring_s.at[s, 1])

    def rms(values, gain):
        return values * lax.rsqrt(jnp.mean(values * values, axis=1, keepdims=True) + 1e-06) * gain

    def f_copy(r):
        rows = pl.ds(pl.multiple_of(me * 8, 8), 8)
        return remote(fs.at[r], fl.at[rows, :], f_s, f_r, (c * Z + z, r))

    def f_self():
        rows = pl.ds(pl.multiple_of(me * 8, 8), 8)
        return pltpu.make_async_copy(fs.at[head], fl.at[rows, :], f_r)

    def f_start():
        for r in range(CHIPS):
            k = r // 2
            first = 384 * (k % 4) + HD * (r % 2)
            fs[r] = xp[8 * (k // 4) : 8 * (k // 4) + 8, first : first + 256]

        def body(o, carry):
            f_copy(lax.rem(head + o, CHIPS)).start()
            return carry

        lax.fori_loop(1, CHIPS, body, 0)

        @pl.when(natural)
        def _():
            f_self().start()

        @pl.when(jnp.logical_not(natural))
        def _():
            f_copy(head).start()

    def f_wait():
        wait_bytes(fl, f_r)
        xt[...] = fl[...].T

    def t_copy(r):
        return remote(tt.at[r], ft.at[me], t_s, t_r, (c * Z + z, r))

    own_rows = pl.ds(pl.multiple_of(own * TOK, 16), TOK)

    for s in range(STEPS):
        qkv = jnp.dot(hb[...], wq[...], preferred_element_type=F32)
        query = rms(qkv[:, 0:HD], gains[0]).astype(BF16)
        fresh = (rms(qkv[:, HD : 2 * HD], gains[1]).astype(BF16), qkv[:, 2 * HD :].astype(BF16))
        if s > 0:
            kv_sent_own(s - 1)
        for i in range(2):
            old = kv[s, i, own_rows, :].astype(F32)
            if s < STEPS - 1:
                change = (fresh[i].astype(F32) - old).astype(BF16)
                kv[s + 1, i, own_rows, :] = (old + change.astype(F32)).astype(BF16)
            kv[s, i, own_rows, :] = fresh[i]
        if s < STEPS - 1:
            kv_start(s)
        if s == 0:
            pair_all(1)
        og[:, HD:512] = jax.nn.gelu(
            jnp.dot(hb[...], wi[...], preferred_element_type=F32), approximate=True
        ).astype(BF16)
        if s == 0:
            ring_end(2)
        else:
            kv_stage(s - 1, 4)
            kv_wait(s - 1)
        top = jnp.full((TOK, 1), -jnp.inf, F32)
        for j in range(KEYS // CHUNK):
            cols = slice(CHUNK * j, CHUNK * j + CHUNK)
            score = lax.dot_general(query, kv[s, 0, cols, :], NT, preferred_element_type=F32)
            score = score * (1.0 / math.sqrt(HD))
            scores[:, cols] = score
            top = jnp.maximum(top, jnp.max(score, axis=1, keepdims=True))
        mass = jnp.zeros((TOK, 1), F32)
        mixed = jnp.zeros((TOK, HD), F32)
        for j in range(KEYS // CHUNK):
            cols = slice(CHUNK * j, CHUNK * j + CHUNK)
            weight = jnp.exp(scores[:, cols] - top)
            mass = mass + jnp.sum(weight, axis=1, keepdims=True)
            mixed = mixed + jnp.dot(weight.astype(BF16), kv[s, 1, cols, :], preferred_element_type=F32)
        og[:, 0:HD] = (mixed / mass).astype(BF16)
        if s == 0:
            pair_all(2)
        elif s < STEPS - 1:
            rs_sent()
        level = [sigma(jnp.full((16, HD), times[s + i].astype(F32))) for i in range(2)]
        gap = (level[1] - level[0])[:, 0:1]
        if s == STEPS - 1:
            break
        for n in range(4):
            half, first = n // 2, 384 * (n % 2)
            cols = slice(384 * n, 384 * n + 384)
            upper = slice(HALF + 384 * n, HALF + 384 * n + 384)
            low = lax.dot_general(og[...], wo[cols, :], NT, preferred_element_type=F32)
            high = lax.dot_general(og[...], wo[upper, :], NT, preferred_element_type=F32)
            for q in range(CHIPS):
                rows = slice(8 * q, 8 * q + 8)
                spot = 16 * (q if half == 0 else 4 * (q % 4) + q // 4)
                both = jnp.concatenate([low[rows], high[rows]], axis=0).astype(BF16)
                tsend[half, spot : spot + 16, first : first + 384] = both
            if n % 2 == 1:
                for d in (1, 3, 2):
                    rs1(s, half, d).start()
        kv_stage(s, 1)
        rs_middle(s)
        kv_stage(s, 2)
        xp[...] = xp[...] + gap * rs_end(s)
        ag_sent(s)
        ag_start(s + 1)
        kv_stage(s, 3)
        ag_forward(s + 1)
        if s == STEPS - 2:
            f_start()
        for half in range(2):
            ag_end(s + 1, half)
            unpack(s + 1, half)

    for g in range(4):
        group = lax.rem(lax.div(head, 4) + g, 4)
        features = pl.ds(pl.multiple_of(group * 768, 16), 768)
        term = lax.dot_general(wo[features, :], og[...], NT, preferred_element_type=F32).astype(BF16)
        for i in range(4):
            r = group * 4 + i
            tt[r] = term[192 * i : 192 * i + 192]

            @pl.when(jnp.logical_and(natural, r == head))
            def _():
                pltpu.make_async_copy(tt.at[r], ft.at[me], t_r).start()

            @pl.when(jnp.logical_not(jnp.logical_and(natural, r == head)))
            def _():
                t_copy(r).start()

    f_wait()
    wait_bytes(ft, t_r)
    total = jnp.zeros((192, TOK), F32)
    for q in range(CHIPS):
        total = total + ft[q].astype(F32)
    out[...] = xt[place, :] + gap[0:1, 0:1] * total

    rs_sent()
    ag_sent(STEPS - 1)
    for s in range(STEPS - 1):
        kv_sent_rest(s)
    for j in range(3):
        wait_bytes(weights[j].at[0 : Z * ROWS, :], pair_s.at[j])
        wait_bytes(weights[j].at[0 : (15 if j > 0 else 13) * ROWS, :], ring_s.at[j])
    wait_bytes(wq.at[0 : 2 * ROWS, :], first_s)

    @pl.when(natural)
    def _():
        wait_bytes(xs.at[0:15], x_s)
        wait_bytes(fs.at[0:15], f_s)
        wait_bytes(tt.at[0:15], t_s)
        wait_bytes(kv.at[0], cache_s.at[0])
        wait_bytes(gains, cache_s.at[1])

    @pl.when(jnp.logical_not(natural))
    def _():
        wait_bytes(xs, x_s)
        wait_bytes(fs, f_s)
        wait_bytes(tt, t_s)
        wait_bytes(wo.at[0:240, :], swap_s)


def on_device(
    state, mod_weight, w_qkv, q_gain, k_gain, w_in, w_attn, w_out, cache_keys, cache_values, timesteps
):
    vmem = pl.BlockSpec(memory_space=pltpu.VMEM)
    hbm = pl.BlockSpec(memory_space=pl.ANY)
    smem = pl.BlockSpec(memory_space=pltpu.SMEM)
    dma = pltpu.SemaphoreType.DMA
    one = pltpu.SemaphoreType.DMA
    result = pl.pallas_call(
        kernel,
        out_shape=jax.ShapeDtypeStruct((192, TOK), F32),
        in_specs=[smem, hbm, hbm, hbm, hbm, hbm, hbm, hbm, hbm, hbm, hbm],
        out_specs=vmem,
        scratch_shapes=[
            pltpu.VMEM((D, 384), BF16),
            pltpu.VMEM((D, 384), BF16),
            pltpu.VMEM((D, 512), BF16),
            pltpu.VMEM((STEPS, 2, KEYS, HD), BF16),
            pltpu.VMEM((STEPS, 2, CHIPS * 16, PART), BF16),
            pltpu.VMEM((STEPS, 2, 3, 64, PART), BF16),
            pltpu.VMEM((STEPS, 2, 3, 16, PART), BF16),
            pltpu.VMEM((2, CHIPS * 16, PART), BF16),
            pltpu.VMEM((2, 64, PART), BF16),
            pltpu.VMEM((TOK, D), BF16),
            pltpu.VMEM((TOK, 512), BF16),
            pltpu.VMEM((TOK, KEYS), F32),
            pltpu.VMEM((CHIPS, 16, 256), F32),
            pltpu.VMEM((CHIPS, 16, 256), F32),
            pltpu.VMEM((CHIPS, 8, 256), F32),
            pltpu.VMEM((TOK, 256), F32),
            pltpu.VMEM((CHIPS, 192, TOK), BF16),
            pltpu.VMEM((CHIPS, 192, TOK), BF16),
            pltpu.VMEM((256, TOK), F32),
            pltpu.VMEM((2, 256, 256), BF16),
            pltpu.VMEM((6, 16, HALF), F32),
            pltpu.VMEM((16, HALF), F32),
            pltpu.VMEM((2, 1, HD), F32),
            dma((2,)), dma((2,)), one, dma((3,)), one, dma((3,)), dma((3, 2, 2, 2)), dma((3,)), dma((3,)),
            dma((2, 2)), dma((2, 2, 4, 2)), dma((2,)), one, one, one, dma((2, 3)), dma((2,)),
            dma((2,)), dma((2,)), dma((2,)), dma((2,)), one, one, one, one, dma((2,)),
        ],
        compiler_params=pltpu.CompilerParams(
            collective_id=0, has_side_effects=True, vmem_limit_bytes=60 * 1024 * 1024
        ),
    )(
        timesteps,
        state.T,
        jnp.transpose(mod_weight, (1, 2, 0)),
        w_qkv.reshape(ROWS, 384),
        w_in,
        w_attn.T,
        w_out.T,
        q_gain,
        k_gain,
        cache_keys.reshape(KEYS, HD),
        cache_values.reshape(KEYS, HD),
    )
    return result.T


def solution(mesh):
    in_specs = (
        P("patch", "head"),
        P(None, None, "head"),
        P("patch", "head", None),
        P("head", None),
        P("head", None),
        P("patch", "head"),
        P("head", "patch"),
        P("head", "patch"),
        P(None, "head", None),
        P(None, "head", None),
        P(),
    )
    return jax.shard_map(
        on_device, mesh=mesh, in_specs=in_specs, out_specs=P("patch", "head"), check_vma=False
    )
```

```python
import math

import jax
import jax.numpy as jnp
from jax import lax
from jax.experimental import pallas as pl
from jax.experimental.pallas import tpu as pltpu
from jax.sharding import PartitionSpec as P

MESH = pl.DeviceIdType.MESH
F32 = jnp.float32
BF16 = jnp.bfloat16
SCHED = 1000
STEPS = 3
Z = 16
CHIPS = 16
TOK = 128
D = 3072
HALF = D // 2
PART = HALF // 2
HD = 128
ROWS = 96
KEYS = 4096
CHUNK = 1024
NT = (((1,), (1,)), ((), ()))


def sigma(unit_index):
    unit = 1.0 - unit_index / SCHED
    return 3.0 * unit / (1.0 + 2.0 * unit)


def kernel(
    times, state, mod_w, w_qkv, w_in, w_attn, w_out, q_gain, k_gain, cache_k, cache_v,
    out,
    wq, wi, wo, kv, hland, r1, r2, tsend, p2, hb, og, scores, xs, xl, fs, fl, tt, ft, xt, mw, modp, xp, gains,
    cache_s, cache_r, swap_s, swap_r, first_s, ring_s, ring_r, pair_s, pair_r,
    kring_s, kring_r, kpair_r, x_s, x_r, ag_s, ag1_r, ag2_r,
    rs1_s, rs1_r, rs2_s, rs2_r, f_s, f_r, t_s, t_r, local,
):
    patch = lax.axis_index("patch")
    head = lax.axis_index("head")
    yl, z = lax.div(patch, Z), lax.rem(patch, Z)
    yh, x, c = lax.div(head, 8), lax.rem(lax.div(head, 2), 4), lax.rem(head, 2)
    y = yh * 2 + yl
    me = y * 4 + x
    own = c * Z + z
    natural = c == yl

    def dev(yy, xx, cc, zz):
        return (lax.rem(yy, 2) * Z + zz, lax.div(yy, 2) * 8 + xx * 2 + cc)

    def chip_at(o):
        return lax.rem(y + lax.div(o, 4), 4), lax.rem(x + lax.rem(o, 4), 4)

    def remote(src, dst, send, recv, device):
        return pltpu.make_async_remote_copy(
            src_ref=src, dst_ref=dst, send_sem=send, recv_sem=recv, device_id=device, device_id_type=MESH
        )

    partner = dev(y, x, 1 - c, z)

    def wait_bytes(block, sem):
        pltpu.make_async_copy(block, block, sem).wait()

    z_next = (dev(y, x, c, lax.rem(z + 1, Z)), dev(y, x, c, lax.rem(z + Z - 1, Z)))
    z_far = (dev(y, x, c, lax.rem(z + 2, Z)), dev(y, x, c, lax.rem(z + Z - 2, Z)))
    twin = dev(yh * 2 + c, x, yl, z)
    twin_next = (dev(yh * 2 + c, x, yl, lax.rem(z + 1, Z)), dev(yh * 2 + c, x, yl, lax.rem(z + Z - 1, Z)))

    barrier = pltpu.get_barrier_semaphore()

    def greet(device):
        pl.semaphore_signal(barrier, inc=1, device_id=device, device_id_type=MESH)

    for device in z_next + z_far + twin_next:
        greet(device)
    rows_y = [lax.rem(y + d, 4) for d in range(4)]
    rows_x = [lax.rem(x + d, 4) for d in range(4)]
    greet(partner)
    for o in range(1, CHIPS):
        for core in range(2):
            greet(dev(rows_y[o // 4], rows_x[o % 4], core, z))

    weights = (wq, wi, wo)

    def slab(j, zz, half=None):
        start, size = (c * Z + zz) * ROWS, ROWS
        if half is not None:
            start, size = start + half * (ROWS // 2), ROWS // 2
        return weights[j].at[pl.ds(pl.multiple_of(start, 16), size), :]

    def shard(i, block):
        rows = pl.ds(pl.multiple_of(block * ROWS, 16), ROWS)
        return (
            (w_qkv, wq.at[rows, :]),
            (w_in, wi.at[rows, :]),
            (w_attn, wo.at[rows, 0:HD]),
            (w_out, wo.at[rows, HD:512]),
        )[i]

    def caches():
        return (
            (cache_k, kv.at[0, 0]),
            (cache_v, kv.at[0, 1]),
            (q_gain, gains.at[0]),
            (k_gain, gains.at[1]),
        )

    place = pl.ds(pl.multiple_of(c * 64, 64), 192)
    mw[...] = jnp.zeros_like(mw)
    xt[...] = jnp.zeros_like(xt)
    loads = [
        pltpu.make_async_copy(state, xt.at[place, :], local.at[0]),
        pltpu.make_async_copy(mod_w, mw.at[:, place, :], local.at[1]),
    ]
    for load in loads:
        load.start()

    pl.semaphore_wait(barrier, 37)

    for half in range(2):
        for d in range(2):
            src = w_qkv.at[half * (ROWS // 2) : (half + 1) * (ROWS // 2), :]
            rows = pl.ds(pl.multiple_of(patch * ROWS + half * (ROWS // 2), 16), ROWS // 2)
            remote(src, wq.at[rows, :], first_s, ring_r.at[0, half, d, 0], twin_next[d]).start()
    part_of = (0, 1, 2, 2)

    @pl.when(natural)
    def _():
        for i in (1, 2, 3, 0):
            src, dst = shard(i, patch)
            pltpu.make_async_copy(src, dst, swap_r.at[part_of[i]]).start()
        for i, (src, dst) in enumerate(caches()):
            pltpu.make_async_copy(src, dst, cache_r.at[i // 2]).start()
            remote(src, dst, cache_s.at[i // 2], cache_r.at[i // 2], partner).start()

    @pl.when(jnp.logical_not(natural))
    def _():
        for i in (1, 2, 3, 0):
            src, dst = shard(i, patch)
            remote(src, dst, swap_s, swap_r.at[part_of[i]], twin).start()

    def pair_copy(j, zz):
        part = slab(j, zz)
        return remote(part, part, pair_s.at[j], pair_r.at[j], partner)

    def ring_copy(j, half, d, k, zz):
        block = slab(j, zz, half)
        return remote(block, block, ring_s.at[j], ring_r.at[j, half, d, lax.rem(k, 2)], z_next[d])

    def source(d, k):
        return lax.rem(z + Z - k, Z) if d == 0 else lax.rem(z + k, Z)

    def ring_start(j):
        wait_bytes(slab(j, z), swap_r.at[j])
        if j > 0:
            for half in range(2):
                for d in range(2):
                    ring_copy(j, half, d, 0, z).start()
        pair_copy(j, z).start()

    def ring_hop(j, k, last=False):
        for half in range(2):
            for d in range(2):
                ring_copy(j, half, d, k - 1, source(d, k)).wait_recv()
            for d in range(2):
                if not last or half == d:
                    ring_copy(j, half, d, k, source(d, k)).start()
        for d in range(2):
            pair_copy(j, source(d, k)).start()

    def ring_end(j):
        zz = source(0, 8)
        for d in range(2):
            ring_copy(j, d, d, 7, zz).wait_recv()
        pair_copy(j, zz).start()

    def pair_all(j):
        rows = pl.ds(pl.multiple_of((1 - c) * Z * ROWS, 16), Z * ROWS)
        wait_bytes(weights[j].at[rows, :], pair_r.at[j])

    for j in (1, 2, 0):
        ring_start(j)

    row = lax.broadcasted_iota(jnp.int32, (8, HD), 0)
    lane = lax.broadcasted_iota(jnp.int32, (8, HD), 1)
    stepped = lax.rem(row, 3)
    when = jnp.zeros((8, HD), F32)
    for s in range(STEPS):
        when = jnp.where(stepped == s, times[s].astype(F32), when)
    freq = jnp.exp(-math.log(10000.0) * lane.astype(F32) / HD)
    angle = 1000.0 * sigma(when) * freq
    emb = jnp.concatenate([jnp.cos(angle), jnp.sin(angle)], axis=1).astype(BF16)
    for load in loads:
        load.wait()
    mods = [lax.dot_general(emb, mw[j], NT, preferred_element_type=F32) for j in range(2)]
    row2 = lax.broadcasted_iota(jnp.int32, (8, 256), 0)
    mod_rows = jnp.where(row2 < 3, mods[0], mods[1])
    rows_here = xt[...].T
    for q in range(CHIPS):
        xs[q, 0:8] = rows_here[8 * q : 8 * q + 8]
        xs[q, 8:16] = mod_rows

    def x_copy(q, device):
        return remote(xs.at[q], xl.at[head], x_s, x_r, device)

    @pl.when(natural)
    def _():
        pltpu.make_async_copy(xs.at[me], xl.at[head], x_r).start()

    @pl.when(jnp.logical_not(natural))
    def _():
        x_copy(me, partner).start()

    def x_start(o, carry):
        yy, xx = chip_at(o)
        x_copy(yy * 4 + xx, dev(yy, xx, yl, z)).start()
        return carry

    lax.fori_loop(1, CHIPS, x_start, 0)

    def hop(k, carry):
        ring_hop(0, k)
        ring_hop(1, k)
        ring_hop(2, k)
        return carry

    ring_hop(0, 1)
    ring_hop(1, 1)
    ring_hop(2, 1)
    lax.fori_loop(2, 4, hop, 0)
    wait_bytes(xl, x_r)
    for k in range(8):
        a, b = xl[2 * k], xl[2 * k + 1]
        group = jnp.concatenate([a[:, :HD], a[:, HD:] + b[:, :HD], b[:, HD:]], axis=1)
        rows, cols = slice(8 * (k // 4), 8 * (k // 4) + 8), slice(384 * (k % 4), 384 * (k % 4) + 384)
        xp[rows, cols] = group[0:8]
        for i in range(6):
            modp[i, rows, cols] = jnp.broadcast_to(group[8 + i : 9 + i], (8, 384))

    def fold(sums):
        total = (sums[0:8] + sums[8:16]) * (1.0 / D)
        return jnp.concatenate([total, total], axis=0)

    def turn(i, d):
        return lax.rem(i + d, 4)

    def slot(yy, xx):
        return pl.ds(pl.multiple_of((yy * 4 + xx) * 16, 16), 16)

    def line(half, d):
        return dev(y, turn(x, d), c, z) if half == 0 else dev(turn(y, d), x, c, z)

    def origin(half, d):
        return slot(y, turn(x, 4 - d)) if half == 0 else slot(turn(y, 4 - d), x)

    def ag1(s, half, d, rows):
        block = hland.at[s, half, rows, :]
        return remote(block, block, ag_s, ag1_r.at[half, d - 1], line(half, d))

    def ag2(s, half, d, rows):
        block = hland.at[s, half, rows, :]
        return remote(block, block, ag_s, ag2_r.at[half], line(1 - half, d))

    def ag_start(s):
        rows = xp[...]
        delta = rows - fold(jnp.sum(rows, axis=1, keepdims=True))
        var = fold(jnp.sum(delta * delta, axis=1, keepdims=True))
        h = (delta * lax.rsqrt(var + 1e-06) * (1.0 + modp[s]) + modp[3 + s]).astype(BF16)
        mine = slot(y, x)
        for half in range(2):
            hland[s, half, mine, :] = h[:, half * PART : half * PART + PART]
        for d in (1, 3, 2):
            for half in range(2):
                ag1(s, half, d, mine).start()
        for d in (1, 3, 2):
            for half in range(2):
                ag2(s, half, d, mine).start()

    def ag_forward(s):
        for d in (1, 3, 2):
            for half in range(2):
                rows = origin(half, d)
                ag1(s, half, d, rows).wait_recv()
                for e in (1, 3, 2):
                    ag2(s, half, e, rows).start()

    def ag_end(s, half):
        wait_bytes(hland.at[s, half, 0:192, :], ag2_r.at[half])

    def ag_sent(s):
        wait_bytes(hland.at[s, :, 0:240, :], ag_s)

    def rs1(s, half, d):
        to = turn(y if half == 0 else x, d)
        block = tsend.at[half, pl.ds(pl.multiple_of(to * 64, 64), 64), :]
        return remote(
            block, r1.at[s, half, d - 1], rs1_s.at[half], rs1_r.at[half], line(1 - half, d)
        )

    def rs2(s, half, d):
        to = turn(x if half == 0 else y, d)
        block = p2.at[half, pl.ds(pl.multiple_of(to * 16, 16), 16), :]
        return remote(
            block, r2.at[s, half, d - 1], rs2_s.at[half], rs2_r.at[half], line(half, d)
        )

    def rs_middle(s):
        for half in range(2):
            here = pl.ds(pl.multiple_of((y if half == 0 else x) * 64, 64), 64)
            wait_bytes(r1.at[s, half], rs1_r.at[half])
            part = tsend[half, here, :].astype(F32)
            for d in range(3):
                part = part + r1[s, half, d].astype(F32)
            p2[half] = part.astype(BF16)
            for d in (1, 3, 2):
                rs2(s, half, d).start()

    def rs_sent():
        for half in range(2):
            wait_bytes(r1.at[0, half], rs1_s.at[half])
            wait_bytes(r2.at[0, half], rs2_s.at[half])

    def rs_end(s):
        parts = []
        for half in range(2):
            here = pl.ds(pl.multiple_of((x if half == 0 else y) * 16, 16), 16)
            wait_bytes(r2.at[s, half], rs2_r.at[half])
            part = p2[half, here, :].astype(F32)
            for d in (1, 3, 2):
                part = part + r2[s, half, d - 1].astype(F32)
            parts.append(part)
        return jnp.concatenate(parts, axis=1)

    def unpack(s, half):
        for m in range(8):
            block = hland[s, half, 32 * m : 32 * m + 32, :].astype(F32)
            rows = slice(16 * m, 16 * m + 16)
            low, high = half * PART, HALF + half * PART
            hb[rows, low : low + PART] = jnp.concatenate([block[0:8], block[16:24]], axis=0).astype(BF16)
            hb[rows, high : high + PART] = jnp.concatenate([block[8:16], block[24:32]], axis=0).astype(BF16)

    ag_start(0)
    lax.fori_loop(4, 5, hop, 0)
    ag_forward(0)
    lax.fori_loop(5, 7, hop, 0)
    for half in range(2):
        ag_end(0, half)
        unpack(0, half)
    ring_hop(0, 7, last=True)
    ring_hop(1, 7, last=True)
    ring_hop(2, 7, last=True)
    ring_end(0)
    ring_end(1)
    pair_all(0)

    wait_bytes(kv.at[0], cache_r.at[0])
    wait_bytes(gains, cache_r.at[1])

    def kv_block(s, cc, zz, part=None):
        start, size = (cc * Z + zz) * TOK, TOK
        if part is not None:
            start, size = start + part * (TOK // 2), TOK // 2
        return kv.at[s + 1, :, pl.ds(pl.multiple_of(start, 16), size), :]

    def kring_copy(s, d, k, far, zz, part=None):
        block = kv_block(s, c, zz, part)
        device = z_far[d] if far else z_next[d]
        return remote(block, block, kring_s.at[s, min(k, 1)], kring_r.at[s, d, k, far], device)

    def kpair_copy(s, zz, rest=1):
        block = kv_block(s, c, zz)
        return remote(block, block, kring_s.at[s, rest], kpair_r.at[s], partner)

    def kv_send(s, k):
        for d in range(2):
            kring_copy(s, d, k, 1, source(d, 2 * k), d if k == 3 else None).start()
        for d in range(2):
            kring_copy(s, d, k, 0, source(d, 2 * k)).start()

    def kv_start(s):
        kv_send(s, 0)
        kpair_copy(s, z, 0).start()

    def kv_stage(s, k):
        for d in range(2):
            kring_copy(s, d, k - 1, 1, source(d, 2 * k), d if k == 4 else None).wait_recv()
        if k < 4:
            kv_send(s, k)
            for d in range(2):
                kpair_copy(s, source(d, 2 * k)).start()
        else:
            kpair_copy(s, source(0, 8)).start()
        for near in (k - 1,):
            for d in range(2):
                zz = source(d, 2 * near + 1)
                kring_copy(s, d, near, 0, zz).wait_recv()
                kpair_copy(s, zz).start()

    def kv_wait(s):
        rows = pl.ds(pl.multiple_of((1 - c) * Z * TOK, 16), Z * TOK)
        wait_bytes(kv.at[s + 1, :, rows, :], kpair_r.at[s])

    def kv_sent_own(s):
        wait_bytes(kv.at[s + 1, :, 0 : 5 * TOK, :], kring_s.at[s, 0])

    def kv_sent_rest(s):
        wait_bytes(kv.at[s + 1, :, 0 : 26 * TOK, :], kring_s.at[s, 1])

    def rms(values, gain):
        return values * lax.rsqrt(jnp.mean(values * values, axis=1, keepdims=True) + 1e-06) * gain

    def f_copy(r):
        rows = pl.ds(pl.multiple_of(me * 8, 8), 8)
        return remote(fs.at[r], fl.at[rows, :], f_s, f_r, (c * Z + z, r))

    def f_self():
        rows = pl.ds(pl.multiple_of(me * 8, 8), 8)
        return pltpu.make_async_copy(fs.at[head], fl.at[rows, :], f_r)

    def f_start():
        for r in range(CHIPS):
            k = r // 2
            first = 384 * (k % 4) + HD * (r % 2)
            fs[r] = xp[8 * (k // 4) : 8 * (k // 4) + 8, first : first + 256]

        def body(o, carry):
            f_copy(lax.rem(head + o, CHIPS)).start()
            return carry

        lax.fori_loop(1, CHIPS, body, 0)

        @pl.when(natural)
        def _():
            f_self().start()

        @pl.when(jnp.logical_not(natural))
        def _():
            f_copy(head).start()

    def f_wait():
        wait_bytes(fl, f_r)
        xt[...] = fl[...].T

    def t_copy(r):
        return remote(tt.at[r], ft.at[me], t_s, t_r, (c * Z + z, r))

    own_rows = pl.ds(pl.multiple_of(own * TOK, 16), TOK)

    for s in range(STEPS):
        both = jnp.dot(hb[...], wq[:, HD:384], preferred_element_type=F32)
        fresh = (rms(both[:, :HD], gains[1]).astype(BF16), both[:, HD:].astype(BF16))
        if s > 0:
            kv_sent_own(s - 1)
        for i in range(2):
            old = kv[s, i, own_rows, :].astype(F32)
            if s < STEPS - 1:
                change = (fresh[i].astype(F32) - old).astype(BF16)
                kv[s + 1, i, own_rows, :] = (old + change.astype(F32)).astype(BF16)
            kv[s, i, own_rows, :] = fresh[i]
        if s < STEPS - 1:
            kv_start(s)
        query = rms(jnp.dot(hb[...], wq[:, 0:HD], preferred_element_type=F32), gains[0]).astype(BF16)
        if s == 0:
            pair_all(1)
        og[:, HD:512] = jax.nn.gelu(
            jnp.dot(hb[...], wi[...], preferred_element_type=F32), approximate=True
        ).astype(BF16)
        if s == 0:
            ring_end(2)
        else:
            kv_stage(s - 1, 4)
            kv_wait(s - 1)
        top = jnp.full((TOK, 1), -jnp.inf, F32)
        for j in range(KEYS // CHUNK):
            cols = slice(CHUNK * j, CHUNK * j + CHUNK)
            score = lax.dot_general(query, kv[s, 0, cols, :], NT, preferred_element_type=F32)
            scores[:, cols] = score
            top = jnp.maximum(top, jnp.max(score, axis=1, keepdims=True))
        mass = jnp.zeros((TOK, 1), F32)
        mixed = jnp.zeros((TOK, HD), F32)
        for j in range(KEYS // CHUNK):
            cols = slice(CHUNK * j, CHUNK * j + CHUNK)
            weight = jnp.exp2((scores[:, cols] - top) * (math.log2(math.e) / math.sqrt(HD)))
            mass = mass + jnp.sum(weight, axis=1, keepdims=True)
            mixed = mixed + jnp.dot(weight.astype(BF16), kv[s, 1, cols, :], preferred_element_type=F32)
        og[:, 0:HD] = (mixed / mass).astype(BF16)
        if s == 0:
            pair_all(2)
        elif s < STEPS - 1:
            rs_sent()
        level = [sigma(jnp.full((16, HD), times[s + i].astype(F32))) for i in range(2)]
        gap = (level[1] - level[0])[:, 0:1]
        if s == STEPS - 1:
            break
        for half in range(2):
            cols = slice(PART * half, PART * half + PART)
            upper = slice(HALF + PART * half, HALF + PART * half + PART)
            low = lax.dot_general(og[...], wo[cols, :], NT, preferred_element_type=F32)
            high = lax.dot_general(og[...], wo[upper, :], NT, preferred_element_type=F32)
            for q in range(CHIPS):
                rows = slice(8 * q, 8 * q + 8)
                spot = 16 * (q if half == 0 else 4 * (q % 4) + q // 4)
                both = jnp.concatenate([low[rows], high[rows]], axis=0).astype(BF16)
                tsend[half, spot : spot + 16, :] = both
            for d in (1, 3, 2):
                rs1(s, half, d).start()
        kv_stage(s, 1)
        rs_middle(s)
        kv_stage(s, 2)
        xp[...] = xp[...] + gap * rs_end(s)
        ag_sent(s)
        ag_start(s + 1)
        kv_stage(s, 3)
        ag_forward(s + 1)
        if s == STEPS - 2:
            f_start()
        for half in range(2):
            ag_end(s + 1, half)
            unpack(s + 1, half)

    for g in range(4):
        group = lax.rem(lax.div(head, 4) + g, 4)
        features = pl.ds(pl.multiple_of(group * 768, 16), 768)
        term = lax.dot_general(wo[features, :], og[...], NT, preferred_element_type=F32).astype(BF16)
        for i in range(4):
            r = group * 4 + i
            tt[r] = term[192 * i : 192 * i + 192]

            @pl.when(jnp.logical_and(natural, r == head))
            def _():
                pltpu.make_async_copy(tt.at[r], ft.at[me], t_r).start()

            @pl.when(jnp.logical_not(jnp.logical_and(natural, r == head)))
            def _():
                t_copy(r).start()

    f_wait()
    wait_bytes(ft, t_r)
    total = jnp.zeros((192, TOK), F32)
    for q in range(CHIPS):
        total = total + ft[q].astype(F32)
    out[...] = xt[place, :] + gap[0:1, 0:1] * total

    rs_sent()
    ag_sent(STEPS - 1)
    for s in range(STEPS - 1):
        kv_sent_rest(s)
    for j in range(3):
        wait_bytes(weights[j].at[0 : Z * ROWS, :], pair_s.at[j])
        wait_bytes(weights[j].at[0 : (15 if j > 0 else 13) * ROWS, :], ring_s.at[j])
    wait_bytes(wq.at[0 : 2 * ROWS, :], first_s)

    @pl.when(natural)
    def _():
        wait_bytes(xs.at[0:15], x_s)
        wait_bytes(fs.at[0:15], f_s)
        wait_bytes(tt.at[0:15], t_s)
        wait_bytes(kv.at[0], cache_s.at[0])
        wait_bytes(gains, cache_s.at[1])

    @pl.when(jnp.logical_not(natural))
    def _():
        wait_bytes(xs, x_s)
        wait_bytes(fs, f_s)
        wait_bytes(tt, t_s)
        wait_bytes(wo.at[0:240, :], swap_s)


def on_device(
    state, mod_weight, w_qkv, q_gain, k_gain, w_in, w_attn, w_out, cache_keys, cache_values, timesteps
):
    vmem = pl.BlockSpec(memory_space=pltpu.VMEM)
    hbm = pl.BlockSpec(memory_space=pl.ANY)
    smem = pl.BlockSpec(memory_space=pltpu.SMEM)
    dma = pltpu.SemaphoreType.DMA
    one = pltpu.SemaphoreType.DMA
    result = pl.pallas_call(
        kernel,
        out_shape=jax.ShapeDtypeStruct((192, TOK), F32),
        in_specs=[smem, hbm, hbm, hbm, hbm, hbm, hbm, hbm, hbm, hbm, hbm],
        out_specs=vmem,
        scratch_shapes=[
            pltpu.VMEM((D, 384), BF16),
            pltpu.VMEM((D, 384), BF16),
            pltpu.VMEM((D, 512), BF16),
            pltpu.VMEM((STEPS, 2, KEYS, HD), BF16),
            pltpu.VMEM((STEPS, 2, CHIPS * 16, PART), BF16),
            pltpu.VMEM((STEPS, 2, 3, 64, PART), BF16),
            pltpu.VMEM((STEPS, 2, 3, 16, PART), BF16),
            pltpu.VMEM((2, CHIPS * 16, PART), BF16),
            pltpu.VMEM((2, 64, PART), BF16),
            pltpu.VMEM((TOK, D), BF16),
            pltpu.VMEM((TOK, 512), BF16),
            pltpu.VMEM((TOK, KEYS), F32),
            pltpu.VMEM((CHIPS, 16, 256), F32),
            pltpu.VMEM((CHIPS, 16, 256), F32),
            pltpu.VMEM((CHIPS, 8, 256), F32),
            pltpu.VMEM((TOK, 256), F32),
            pltpu.VMEM((CHIPS, 192, TOK), BF16),
            pltpu.VMEM((CHIPS, 192, TOK), BF16),
            pltpu.VMEM((256, TOK), F32),
            pltpu.VMEM((2, 256, 256), BF16),
            pltpu.VMEM((6, 16, HALF), F32),
            pltpu.VMEM((16, HALF), F32),
            pltpu.VMEM((2, 1, HD), F32),
            dma((2,)), dma((2,)), one, dma((3,)), one, dma((3,)), dma((3, 2, 2, 2)), dma((3,)), dma((3,)),
            dma((2, 2)), dma((2, 2, 4, 2)), dma((2,)), one, one, one, dma((2, 3)), dma((2,)),
            dma((2,)), dma((2,)), dma((2,)), dma((2,)), one, one, one, one, dma((2,)),
        ],
        compiler_params=pltpu.CompilerParams(
            collective_id=0, has_side_effects=True, vmem_limit_bytes=60 * 1024 * 1024
        ),
    )(
        timesteps,
        state.T,
        jnp.transpose(mod_weight, (1, 2, 0)),
        w_qkv.reshape(ROWS, 384),
        w_in,
        w_attn.T,
        w_out.T,
        q_gain,
        k_gain,
        cache_keys.reshape(KEYS, HD),
        cache_values.reshape(KEYS, HD),
    )
    return result.T


def solution(mesh):
    in_specs = (
        P("patch", "head"),
        P(None, None, "head"),
        P("patch", "head", None),
        P("head", None),
        P("head", None),
        P("patch", "head"),
        P("head", "patch"),
        P("head", "patch"),
        P(None, "head", None),
        P(None, "head", None),
        P(),
    )
    return jax.shard_map(
        on_device, mesh=mesh, in_specs=in_specs, out_specs=P("patch", "head"), check_vma=False
    )
```
